256 devices in a mesh: ctx: 64 (over y_lo, x, z), hid: 4 (over y_hi, core).
Axes of the slice: x: 4, y: 4 (y_hi: 2, y_lo: 2; y = y_hi * 2 + y_lo), z: 8, core: 2. Of those that a mesh axis runs over, the one named last changes fastest.
Arguments:
- activations: bfloat16 [16384, 4096], P('ctx'), may hold values from -6 to 6
- w_in: bfloat16 [3, 4096, 4096], P(None, 'ctx', 'hid'), may hold values from -0.09375 to 0.09375
- short_taps: float32 [3, 4096, 3], P(None, 'hid'), may hold values from -3 to 3
- long_filter: float32 [4096, 16384], P('hid', 'ctx')
- w_out: bfloat16 [4096, 4096], P('hid'), may hold values from -0.09375 to 0.09375
Outputs:
- layer_out: bfloat16 [16384, 4096], P('ctx', 'hid')
The draws below stay inside these ranges and needn't reach their ends.
All inputs are finite; a program needn't handle non-finite values.
Results may differ from the reference program's by a relative error of at most 0.015.
Values may be sent and summed in bfloat16 or wider, within the bound.
A program may use at most 128 MiB of HBM per device.

```python
import math
import jax
import jax.numpy as jnp

D = 4096
C = 4096
TAPS = 3
L_DEV = 256
SEQ = 16384


def draw_long_filter(key, part):
    key = jax.random.fold_in(key, 11)
    key_pick, key_slow, key_fast, key_noise = jax.random.split(key, 4)
    share = 0.5
    noise = jax.random.normal(key_noise, (C, SEQ), jnp.float32)
    slow = jax.random.uniform(key_pick, (C, 1), jnp.float32) < share
    slow_rate = jnp.exp(jax.random.uniform(key_slow, (C, 1), jnp.float32, math.log(0.1 / SEQ), math.log(2.0 / SEQ)))
    fast_rate = jnp.exp(jax.random.uniform(key_fast, (C, 1), jnp.float32, math.log(1.0 / 30.0), math.log(8.0 / L_DEV)))
    rate = jnp.where(slow, slow_rate, fast_rate)
    amplitude = jnp.sqrt((1.0 - jnp.exp(-2.0 * rate)) / (1.0 - jnp.exp(-2.0 * rate * SEQ)))
    lags = jnp.arange(SEQ, dtype=jnp.float32)[None, :]
    return noise * amplitude * jnp.exp(-rate * lags)


def steps_of(rng, dims, pieces, smallest, high):
    gain, own = 1.0, jax.random.fold_in(rng, 6)
    for dim, blocks in pieces:
        steps = jnp.exp(jax.random.uniform(jax.random.fold_in(own, dim), (blocks,), jnp.float32, smallest / len(pieces), high / len(pieces)))
        gain = gain * jnp.repeat(steps, dims[dim] // blocks).reshape([-1 if axis == dim else 1 for axis in range(len(dims))])
    return gain


def normal_values(rng, extent, spread, limit, pieces=(), held_as=jnp.bfloat16):
    values = spread * jax.random.normal(rng, extent, jnp.float32)
    if pieces:
        values = values * steps_of(rng, extent, pieces, -0.22, 0.18)
    return jnp.clip(values, -limit, limit).astype(held_as)


def setup_inputs(seed: int = 0) -> dict:
    arg_keys = jax.random.split(jax.random.key(seed), 6)
    activations = normal_values(arg_keys[0], (SEQ, D), 1.0, 6.0, ((0, 64),))
    w_in = normal_values(arg_keys[1], (3, D, C), D ** -0.5, 0.09375, ((1, 64), (2, 4)))
    short_taps = normal_values(arg_keys[2], (3, C, TAPS), 0.6, 3.0, ((1, 4),), jnp.float32)
    long_filter = draw_long_filter(jax.random.fold_in(arg_keys[5], 71), 0)
    w_out = normal_values(arg_keys[4], (C, D), C ** -0.5, 0.09375, ((0, 4),))
    return {"activations": activations, "w_in": w_in, "short_taps": short_taps, "long_filter": long_filter, "w_out": w_out}


def reference(activations, w_in, short_taps, long_filter, w_out):
    parts = []
    for branch in range(3):
        product = jnp.dot(activations, w_in[branch], preferred_element_type=jnp.float32)
        parts.append(product.astype(jnp.bfloat16).T)
    branches = jnp.stack(parts).astype(jnp.float32)
    padded = jnp.pad(branches, ((0, 0), (0, 0), (TAPS - 1, 0)))
    filtered = jnp.zeros_like(branches)
    for lag in range(TAPS):
        begin = TAPS - 1 - lag
        filtered = filtered + short_taps[:, :, lag][:, :, None] * padded[:, :, begin:begin + SEQ]
    driven = filtered[0] * filtered[2]
    period = 2 * SEQ
    spectrum = jnp.fft.rfft(driven, n=period, axis=1) * jnp.fft.rfft(long_filter, n=period, axis=1)
    convolved = jnp.fft.irfft(spectrum, n=period, axis=1)[:, :SEQ]
    gated = (filtered[1] * convolved).astype(jnp.bfloat16)
    return jnp.dot(gated.T, w_out, preferred_element_type=jnp.float32).astype(jnp.bfloat16)
```

```python
import math

import numpy as np
import ml_dtypes
import jax
import jax.numpy as jnp
from jax import lax
from jax.experimental import pallas as pl
from jax.experimental.pallas import tpu as pltpu
from jax.sharding import PartitionSpec as P

MESH = pl.DeviceIdType.MESH
BF = jnp.bfloat16
F32 = jnp.float32
TAPS = 3
NY, NX, NZ = 2, 4, 8
BLK = 256
HALO = 16
ROWS = BLK + HALO
D = 4096
CQ = 256
DB = 64


def place():
    ctx = lax.axis_index("ctx")
    hid = lax.axis_index("hid")
    yl = lax.div(ctx, 32)
    x = lax.rem(lax.div(ctx, 8), 4)
    z = lax.rem(ctx, 8)
    return ctx, hid, yl, x, z


def at_ctx(yl, x, z):
    return {"ctx": yl * 32 + x * 8 + z}


class Copies:
    def __init__(self, send, recv):
        self.send, self.recv, self.all = send, recv, []

    def start(self, src, dst, device):
        k = len(self.all)
        copy = pltpu.make_async_remote_copy(
            src_ref=src,
            dst_ref=dst,
            send_sem=self.send.at[k],
            recv_sem=self.recv.at[k],
            device_id=device,
            device_id_type=MESH,
        )
        copy.start()
        self.all.append(copy)
        return copy

    def wait_sends(self):
        for copy in self.all:
            copy.wait_send()


N_COPIES = 64


def project_kernel(act, w, taps, drv, qry, abuf, wbuf, bs, local_sem, send_sem, recv_sem):
    ctx, hid, yl, x, z = place()
    core = lax.rem(hid, 2)
    mate = {"hid": hid + 1 - 2 * core}
    right, left = lax.rem(z + 1, NZ), lax.rem(z + NZ - 1, NZ)
    xr, xl, xo = lax.rem(x + 1, NX), lax.rem(x + 3, NX), lax.rem(x + 2, NX)
    after, before = lax.rem(ctx + 1, 64), lax.rem(ctx + 63, 64)
    to_r, to_l = at_ctx(yl, x, right), at_ctx(yl, x, left)
    to_y = at_ctx(1 - yl, x, z)
    to_xr, to_xl, to_xo = at_ctx(yl, xr, z), at_ctx(yl, xl, z), at_ctx(yl, xo, z)

    own_w = pltpu.make_async_copy(
        w.at[:, :, pl.ds(pl.multiple_of(x * CQ, CQ), CQ)], wbuf.at[:, yl, x, z], local_sem.at[0]
    )
    own_a = pltpu.make_async_copy(act, abuf.at[x, pl.ds(HALO, BLK)], local_sem.at[1])
    own_w.start()
    own_a.start()

    barrier = pltpu.get_barrier_semaphore()
    for peer in (to_r, to_l, to_y, to_xr, to_xl, to_xo, mate, {"ctx": after}, {"ctx": before}):
        pl.semaphore_signal(barrier, inc=1, device_id=peer, device_id_type=MESH)
    pl.semaphore_wait(barrier, 9)

    go = Copies(send_sem, recv_sem)
    first = []
    for xp, to in ((xr, to_xr), (xl, to_xl), (xo, to_xo)):
        first.append(
            go.start(w.at[:, :, pl.ds(pl.multiple_of(xp * CQ, CQ), CQ)], wbuf.at[:, yl, x, z], to)
        )
    x_next = lax.rem(lax.div(after, 8), 4)
    halo_in = go.start(act.at[pl.ds(BLK - HALO, HALO)], abuf.at[x_next, pl.ds(0, HALO)], {"ctx": after})

    def a_rows(part):
        return pl.multiple_of(core * 128 + part * 64, 64)

    def a_slot(block, part, count=64):
        return abuf.at[block, pl.ds(pl.multiple_of(HALO + core * 128 + part * 64, 16), count)]

    a_in = []
    for part, to in ((0, to_xr), (1, to_xl), (1, to_xr), (0, to_xl)):
        a_in.append(go.start(act.at[pl.ds(a_rows(part), 64)], a_slot(x, part), to))

    own_w.wait()
    for copy in first:
        copy.wait_recv()

    def piece(index, zs):
        if index == 0:
            return wbuf.at[:, yl, pl.ds(0, 2), zs]
        if index == 1:
            return wbuf.at[:, yl, pl.ds(2, 2), zs]
        if index == 2:
            return wbuf.at[:, 1 - yl, pl.ds(0, 2), zs]
        return wbuf.at[:, yl, pl.ds(index - 1, 1), zs]

    def send(index, zs, to):
        part = piece(index, zs)
        return go.start(part, part, to)

    y_in = [send(0, z, to_y)]
    from_l, from_r = {}, {}
    for index in (0, 1):
        from_l[index, 1] = send(index, z, to_r)
        from_r[index, 1] = send(index, z, to_l)
    y_in.append(send(1, z, to_y))
    y_in[0].wait_recv()
    from_l[2, 1] = send(2, z, to_r)
    from_r[2, 1] = send(2, z, to_l)

    def relay(step):
        zl, zr = lax.rem(z + NZ - step, NZ), lax.rem(z + step, NZ)
        for index in (0, 1, 2):
            from_l[index, step].wait_recv()
            if step < 3:
                from_l[index, step + 1] = send(index, zl, to_r)
            elif index == 0:
                from_l[0, 4] = send(0, zl, to_r)
            elif index == 1:
                from_l[1, 4] = send(3, zl, to_r)
            from_r[index, step].wait_recv()
            if step < 3:
                from_r[index, step + 1] = send(index, zr, to_l)
            elif index == 1:
                from_r[1, 4] = send(4, zr, to_l)
            elif index == 2:
                from_r[2, 4] = send(2, zr, to_l)
            if index == 1:
                y_in.append(send(1, zl, to_y))
                y_in.append(send(1, zr, to_y))

    relay(1)
    a_in[0].wait_recv()
    far = [go.start(a_slot(xl, 0), a_slot(xl, 0), to_xr)]
    a_in[1].wait_recv()
    far.append(go.start(a_slot(xr, 1), a_slot(xr, 1), to_xl))
    halo_in.wait_recv()
    halos = [
        go.start(abuf.at[x, pl.ds(0, HALO)], abuf.at[x, pl.ds(0, HALO)], to) for to in (to_xr, to_xl, to_xo)
    ]
    relay(2)
    a_in[2].wait_recv()
    mates = [go.start(a_slot(xl, 0, 128), a_slot(xl, 0, 128), mate)]
    a_in[3].wait_recv()
    mates.append(go.start(a_slot(xr, 0, 128), a_slot(xr, 0, 128), mate))
    relay(3)
    far[0].wait_recv()
    mates.append(go.start(a_slot(xo, 0), a_slot(xo, 0), mate))
    far[1].wait_recv()
    mates.append(go.start(a_slot(xo, 1), a_slot(xo, 1), mate))
    zo = lax.rem(z + 4, NZ)
    from_l[1, 4].wait_recv()
    y_in.append(send(3, zo, to_y))
    from_r[1, 4].wait_recv()
    y_in.append(send(4, zo, to_y))
    from_l[0, 4].wait_recv()
    from_r[2, 4].wait_recv()
    for copy in y_in[1:] + halos + mates:
        copy.wait_recv()
    own_a.wait()

    def block(xb, carry):
        keep = jnp.where(yl * 32 + xb * 8 + z == 0, 0.0, 1.0).astype(F32)
        a = abuf[xb]
        filtered = []
        for j in range(3):
            wj = wbuf[j].reshape(D, CQ)
            bs[j] = jnp.dot(a, wj, preferred_element_type=F32).astype(BF).astype(F32)
            bs[j, pl.ds(0, HALO)] = bs[j, pl.ds(0, HALO)] * keep
            total = taps[x, 3 * j][None, :] * bs[j, pl.ds(HALO, BLK)]
            for k in range(1, TAPS):
                total = total + taps[x, 3 * j + k][None, :] * bs[j, pl.ds(HALO - k, BLK)]
            filtered.append(total)
        drv[:, xb] = (filtered[0] * filtered[2]).T.astype(BF).reshape(16, 16, BLK)
        qry[xb] = filtered[1].T
        return carry

    lax.fori_loop(0, NX, block, 0)
    go.wait_sends()


def project(act, w, taps):
    return pl.pallas_call(
        project_kernel,
        out_shape=(
            jax.ShapeDtypeStruct((16, NX, 16, BLK), BF),
            jax.ShapeDtypeStruct((NX, CQ, BLK), F32),
        ),
        in_specs=[
            pl.BlockSpec(memory_space=pl.ANY),
            pl.BlockSpec(memory_space=pl.ANY),
            pl.BlockSpec(memory_space=pltpu.VMEM),
        ],
        out_specs=(pl.BlockSpec(memory_space=pltpu.VMEM), pl.BlockSpec(memory_space=pltpu.VMEM)),
        scratch_shapes=[
            pltpu.VMEM((NX, ROWS, D), BF),
            pltpu.VMEM((3, NY, NX, NZ, DB, CQ), BF),
            pltpu.VMEM((3, ROWS, CQ), F32),
            pltpu.SemaphoreType.DMA((2,)),
            pltpu.SemaphoreType.DMA((N_COPIES,)),
            pltpu.SemaphoreType.DMA((N_COPIES,)),
        ],
        compiler_params=pltpu.CompilerParams(
            collective_id=0, has_side_effects=True, vmem_limit_bytes=56 * 1024 * 1024
        ),
        name="project",
    )(act, w, taps)


def halves(table):
    high = table.astype(ml_dtypes.bfloat16)
    low = (table - high.astype(np.float64)).astype(ml_dtypes.bfloat16)
    return high, low


def tables():
    order = np.array([yl * 32 + x * 8 + z for yl in range(NY) for z in range(NZ) for x in range(NX)])
    k1 = np.arange(64) + 0.5
    angle = 2 * np.pi * np.outer(k1, np.arange(64)) / 128
    ahead = np.concatenate([np.cos(angle), -np.sin(angle)], axis=0)
    back = np.concatenate([np.cos(angle.T), -np.sin(angle.T)], axis=1) * 2.0**-14
    turn = 2 * np.pi * np.outer(k1, np.arange(BLK)) / 32768
    inner = 2 * np.pi * (np.outer(np.arange(BLK), np.arange(BLK)) % BLK) / BLK
    c, s = np.cos(inner), np.sin(inner)
    wide = np.block([[c, -s], [s, c]])
    ahead_h, ahead_l = halves(ahead[:, order])
    back_h, back_l = halves(back[order])
    wide_h, wide_l = halves(wide)
    return (
        np.concatenate([ahead_h, ahead_l], axis=1),
        np.stack([np.cos(turn), -np.sin(turn)]).astype(np.float32),
        wide_h,
        wide_l,
        np.concatenate([back_h, back_h, back_l], axis=1),
    )


GROUP = 4


def split(value):
    high = value.astype(BF)
    return high, (value - high.astype(F32)).astype(BF)


def convolve_kernel(sig, flt, ahead, turn, wide_h, wide_l, back, out, wide_sig, wide_flt, out32):
    for source, wide in ((sig, wide_sig), (flt, wide_flt)):
        for side in range(2):
            wide[side] = source[:, :, 128 * side : 128 * side + 128].astype(F32).reshape(1024, 128)

    def inner(value):
        high, low = split(value)
        return (
            jnp.dot(high, wide_h[...], preferred_element_type=F32)
            + jnp.dot(low, wide_h[...], preferred_element_type=F32)
            + jnp.dot(high, wide_l[...], preferred_element_type=F32)
        )

    def spectrum(source, first):
        parts = []
        for i in range(GROUP):
            rows = jnp.concatenate(
                [source[side, pl.ds(first + i, 64, stride=16), :] for side in range(2)], axis=1
            ).astype(BF)
            both = jnp.dot(ahead[...], jnp.concatenate([rows, rows], axis=0), preferred_element_type=F32)
            re, im = both[:64], both[64:]
            parts.append(
                jnp.concatenate([re * turn[0] - im * turn[1], re * turn[1] + im * turn[0]], axis=1)
            )
        return inner(jnp.concatenate(parts, axis=0))

    def group(g, carry):
        first = g * GROUP
        s = spectrum(wide_sig, first)
        h = spectrum(wide_flt, first)
        sr, si, hr, hi = s[:, :BLK], s[:, BLK:], h[:, :BLK], h[:, BLK:]
        product = jnp.concatenate([sr * hr - si * hi, -(sr * hi + si * hr)], axis=1)
        v = inner(product)
        for i in range(GROUP):
            re, im = v[64 * i : 64 * i + 64, :BLK], -v[64 * i : 64 * i + 64, BLK:]
            both = jnp.concatenate([re * turn[0] + im * turn[1], im * turn[0] - re * turn[1]], axis=0)
            high, low = split(both)
            y = jnp.dot(back[...], jnp.concatenate([high, low, high], axis=0), preferred_element_type=F32)
            for side in range(2):
                out32[side, pl.ds(first + i, 64, stride=16), :] = y[:, 128 * side : 128 * side + 128]
        return carry

    lax.fori_loop(0, 16 // GROUP, group, 0)
    for side in range(2):
        out[:, :, 128 * side : 128 * side + 128] = out32[side].reshape(64, 16, 128).astype(BF)


def convolve(sig, flt):
    return pl.pallas_call(
        convolve_kernel,
        out_shape=jax.ShapeDtypeStruct((64, 16, BLK), BF),
        in_specs=[pl.BlockSpec(memory_space=pltpu.VMEM)] * 7,
        out_specs=pl.BlockSpec(memory_space=pltpu.VMEM),
        scratch_shapes=[pltpu.VMEM((2, 1024, 128), F32)] * 3,
        compiler_params=pltpu.CompilerParams(vmem_limit_bytes=48 * 1024 * 1024),
        name="convolve",
    )(sig, flt, *[jnp.asarray(table) for table in tables()])


GROUPS_YZ = [[yl * 32 + x * 8 + z for yl in range(NY) for z in range(NZ)] for x in range(NX)]
GROUPS_X = [[yl * 32 + x * 8 + z for x in range(NX)] for yl in range(NY) for z in range(NZ)]


def on_device(activations, w_in, short_taps, long_filter, w_out):
    filters = long_filter.astype(BF).reshape(NX, NY * NZ, 16, BLK)
    filters = lax.all_to_all(filters, "ctx", 0, 0, axis_index_groups=GROUPS_X, tiled=True)
    filters = lax.all_to_all(filters, "ctx", 1, 1, axis_index_groups=GROUPS_YZ, tiled=True)
    filters = filters.transpose(1, 0, 2, 3).reshape(64, 16, BLK)
    taps = short_taps.transpose(0, 2, 1).reshape(9, NX, CQ).transpose(1, 0, 2)
    driven, query = project(activations, w_in, taps)
    signal = lax.all_to_all(driven, "ctx", 0, 0, axis_index_groups=GROUPS_YZ, tiled=True)
    result = convolve(signal.reshape(64, 16, BLK), filters).reshape(16, NX, 16, BLK)
    result = lax.all_to_all(result, "ctx", 0, 0, axis_index_groups=GROUPS_YZ, tiled=True)
    convolved = result.transpose(1, 0, 2, 3).reshape(NX, CQ, BLK)
    gated = (query * convolved.astype(F32)).astype(BF)
    gated = lax.all_to_all(gated, "ctx", 0, 0, axis_index_groups=GROUPS_X, tiled=True).reshape(1024, BLK)
    partial = jnp.einsum("cd,ct->dt", w_out, gated, preferred_element_type=F32).astype(BF)
    result = lax.psum_scatter(partial, "hid", scatter_dimension=0, tiled=True)
    return result.T


def solution(mesh):
    return jax.shard_map(
        on_device,
        mesh=mesh,
        in_specs=(
            P("ctx", None),
            P(None, "ctx", "hid"),
            P(None, "hid", None),
            P("hid", "ctx"),
            P("hid", None),
        ),
        out_specs=P("ctx", "hid"),
        check_vma=False,
    )
```

```python
import math

import numpy as np
import ml_dtypes
import jax
import jax.numpy as jnp
from jax import lax
from jax.experimental import pallas as pl
from jax.experimental.pallas import tpu as pltpu
from jax.sharding import PartitionSpec as P

MESH = pl.DeviceIdType.MESH
BF = jnp.bfloat16
F32 = jnp.float32
TAPS = 3
NY, NX, NZ = 2, 4, 8
BLK = 256
HALO = 16
ROWS = BLK + HALO
D = 4096
CQ = 256
DB = 64


def place():
    ctx = lax.axis_index("ctx")
    hid = lax.axis_index("hid")
    yl = lax.div(ctx, 32)
    x = lax.rem(lax.div(ctx, 8), 4)
    z = lax.rem(ctx, 8)
    return ctx, hid, yl, x, z


def at_ctx(yl, x, z):
    return {"ctx": yl * 32 + x * 8 + z}


class Copies:
    def __init__(self, send, recv):
        self.send, self.recv, self.all = send, recv, []

    def start(self, src, dst, device):
        k = len(self.all)
        copy = pltpu.make_async_remote_copy(
            src_ref=src,
            dst_ref=dst,
            send_sem=self.send.at[k],
            recv_sem=self.recv.at[k],
            device_id=device,
            device_id_type=MESH,
        )
        copy.start()
        self.all.append(copy)
        return copy

    def wait_sends(self):
        for copy in self.all:
            copy.wait_send()


def halves(table):
    high = table.astype(ml_dtypes.bfloat16)
    low = (table - high.astype(np.float64)).astype(ml_dtypes.bfloat16)
    return high, low


def tables():
    order = np.array([yl * 32 + x * 8 + z for yl in range(NY) for z in range(NZ) for x in range(NX)])
    k1 = np.arange(64) + 0.5
    angle = 2 * np.pi * np.outer(k1, np.arange(64)) / 128
    ahead = np.concatenate([np.cos(angle), -np.sin(angle)], axis=0)
    back = np.concatenate([np.cos(angle.T), -np.sin(angle.T)], axis=1) * 2.0**-14
    turn = 2 * np.pi * np.outer(k1, np.arange(BLK)) / 32768
    inner = 2 * np.pi * (np.outer(np.arange(BLK), np.arange(BLK)) % BLK) / BLK
    c, s = np.cos(inner), np.sin(inner)
    wide = np.block([[c, -s], [s, c]])
    ahead_h, ahead_l = halves(ahead[:, order])
    back_h, back_l = halves(back[order])
    wide_h, wide_l = halves(wide)
    return (
        np.concatenate([ahead_h, ahead_l], axis=1),
        np.stack([np.cos(turn), -np.sin(turn)]).astype(np.float32),
        wide_h,
        wide_l,
        np.concatenate([back_h, back_h, back_l], axis=1),
    )


N_COPIES = 64
GROUP = 4


def split(value):
    high = value.astype(BF)
    return high, (value - high.astype(F32)).astype(BF)


def layer_kernel(
    act, w, taps, flt, w_out, ahead, turn, wide_h, wide_l, back, out,
    abuf, wbuf, bs, f32buf, f16buf, fx, frecv, drv, drecv, qry, qrecv, wide, out32, spec, osend, crecv,
    obuf, psend, precv, ysend, yrecv, local_sem, own_sem, all_send, all_recv, send_sem, recv_sem,
):
    ctx, hid, yl, x, z = place()
    core = lax.rem(hid, 2)
    yh = lax.div(hid, 2)
    mate = {"hid": hid + 1 - 2 * core}
    across = {"hid": lax.rem(hid + 2, 4)}
    me = yl * NZ + z
    right, left = lax.rem(z + 1, NZ), lax.rem(z + NZ - 1, NZ)
    xr, xl, xo = lax.rem(x + 1, NX), lax.rem(x + 3, NX), lax.rem(x + 2, NX)
    after = lax.rem(ctx + 1, 64)
    to_r, to_l = at_ctx(yl, x, right), at_ctx(yl, x, left)
    to_y = at_ctx(1 - yl, x, z)
    to_xr, to_xl, to_xo = at_ctx(yl, xr, z), at_ctx(yl, xl, z), at_ctx(yl, xo, z)

    own_w = pltpu.make_async_copy(
        w.at[:, :, pl.ds(pl.multiple_of(x * CQ, CQ), CQ)], wbuf.at[:, yl, x, z], local_sem.at[0]
    )
    own_a = pltpu.make_async_copy(act, abuf.at[x, pl.ds(HALO, BLK)], local_sem.at[1])
    own_w.start()
    own_a.start()

    own_f = pltpu.make_async_copy(flt, f32buf, local_sem.at[2])
    own_f.start()
    own_o = [
        pltpu.make_async_copy(w_out.at[:, pl.ds(1024 * h, 1024)], obuf.at[h], local_sem.at[3 + h])
        for h in range(4)
    ]
    for copy in own_o:
        copy.start()

    barrier = pltpu.get_barrier_semaphore()

    def greet(t, carry):
        pl.semaphore_signal(barrier, inc=1, device_id={"ctx": lax.rem(ctx + t, 64)}, device_id_type=MESH)
        return carry

    lax.fori_loop(1, 64, greet, 0)
    for peer in (mate, across):
        pl.semaphore_signal(barrier, inc=1, device_id=peer, device_id_type=MESH)
    pl.semaphore_wait(barrier, 65)

    go = Copies(send_sem, recv_sem)

    def spread(src, dst, sem):
        def one(t, carry):
            p = lax.rem(me + t, 16)
            pltpu.make_async_remote_copy(
                src_ref=src(p),
                dst_ref=dst,
                send_sem=all_send.at[sem],
                recv_sem=all_recv.at[sem],
                device_id=at_ctx(lax.div(p, NZ), x, lax.rem(p, NZ)),
                device_id_type=MESH,
            ).start()
            return carry

        lax.fori_loop(1, 16, one, 0)

    def to_all(src, dst, sem):
        spread(lambda p: src.at[p], dst.at[me], sem)
        pltpu.make_async_copy(src.at[me], dst.at[me], own_sem.at[sem]).start()

    def await_all(src, dst, sem):
        pltpu.make_async_copy(src.at[me], dst.at[me], own_sem.at[sem]).wait()
        pltpu.make_async_copy(dst.at[pl.ds(0, 15)], dst.at[pl.ds(0, 15)], all_recv.at[sem]).wait()

    def sent_all(src, sem, count=15):
        pltpu.make_async_copy(src.at[pl.ds(0, count)], src.at[pl.ds(0, count)], all_send.at[sem]).wait()

    first = []
    for xp, to in ((xr, to_xr), (xl, to_xl), (xo, to_xo)):
        first.append(
            go.start(w.at[:, :, pl.ds(pl.multiple_of(xp * CQ, CQ), CQ)], wbuf.at[:, yl, x, z], to)
        )
    x_next = lax.rem(lax.div(after, 8), 4)
    halo_in = go.start(act.at[pl.ds(BLK - HALO, HALO)], abuf.at[x_next, pl.ds(0, HALO)], {"ctx": after})

    def a_rows(part):
        return pl.multiple_of(core * 128 + part * 64, 64)

    def a_slot(block, part, count=64):
        return abuf.at[block, pl.ds(pl.multiple_of(HALO + core * 128 + part * 64, 16), count)]

    a_in = []
    for part, to in ((0, to_xr), (1, to_xl), (1, to_xr), (0, to_xl)):
        a_in.append(go.start(act.at[pl.ds(a_rows(part), 64)], a_slot(x, part), to))

    own_f.wait()
    f16buf[...] = f32buf[...].astype(BF).reshape(NX, 16, 16, BLK)
    own_x = pltpu.make_async_copy(f16buf.at[x], fx.at[:, x], local_sem.at[2])
    own_x.start()
    fx_in = [go.start(f16buf.at[xp], fx.at[:, x], to) for xp, to in ((xr, to_xr), (xl, to_xl), (xo, to_xo))]

    own_w.wait()
    for copy in first:
        copy.wait_recv()

    def piece(index, zs):
        if index == 0:
            return wbuf.at[:, yl, pl.ds(0, 2), zs]
        if index == 1:
            return wbuf.at[:, yl, pl.ds(2, 2), zs]
        if index == 2:
            return wbuf.at[:, 1 - yl, pl.ds(0, 2), zs]
        return wbuf.at[:, yl, pl.ds(index - 1, 1), zs]

    def send(index, zs, to):
        part = piece(index, zs)
        return go.start(part, part, to)

    y_in = [send(0, z, to_y)]
    from_l, from_r = {}, {}
    for index in (0, 1):
        from_l[index, 1] = send(index, z, to_r)
        from_r[index, 1] = send(index, z, to_l)
    y_in.append(send(1, z, to_y))
    y_in[0].wait_recv()
    from_l[2, 1] = send(2, z, to_r)
    from_r[2, 1] = send(2, z, to_l)

    def relay(step):
        zl, zr = lax.rem(z + NZ - step, NZ), lax.rem(z + step, NZ)
        for index in (0, 1, 2):
            from_l[index, step].wait_recv()
            if step < 3:
                from_l[index, step + 1] = send(index, zl, to_r)
            elif index == 0:
                from_l[0, 4] = send(0, zl, to_r)
            elif index == 1:
                from_l[1, 4] = send(3, zl, to_r)
            from_r[index, step].wait_recv()
            if step < 3:
                from_r[index, step + 1] = send(index, zr, to_l)
            elif index == 1:
                from_r[1, 4] = send(4, zr, to_l)
            elif index == 2:
                from_r[2, 4] = send(2, zr, to_l)
            if index == 1:
                y_in.append(send(1, zl, to_y))
                y_in.append(send(1, zr, to_y))

    relay(1)
    a_in[0].wait_recv()
    far = [go.start(a_slot(xl, 0), a_slot(xl, 0), to_xr)]
    a_in[1].wait_recv()
    far.append(go.start(a_slot(xr, 1), a_slot(xr, 1), to_xl))
    halo_in.wait_recv()
    halos = [
        go.start(abuf.at[x, pl.ds(0, HALO)], abuf.at[x, pl.ds(0, HALO)], to) for to in (to_xr, to_xl, to_xo)
    ]
    relay(2)
    a_in[2].wait_recv()
    mates = [go.start(a_slot(xl, 0, 128), a_slot(xl, 0, 128), mate)]
    a_in[3].wait_recv()
    mates.append(go.start(a_slot(xr, 0, 128), a_slot(xr, 0, 128), mate))
    relay(3)
    far[0].wait_recv()
    mates.append(go.start(a_slot(xo, 0), a_slot(xo, 0), mate))
    far[1].wait_recv()
    mates.append(go.start(a_slot(xo, 1), a_slot(xo, 1), mate))
    zo = lax.rem(z + 4, NZ)
    from_l[1, 4].wait_recv()
    y_in.append(send(3, zo, to_y))
    from_r[1, 4].wait_recv()
    y_in.append(send(4, zo, to_y))
    from_l[0, 4].wait_recv()
    from_r[2, 4].wait_recv()
    own_x.wait()
    for copy in fx_in:
        copy.wait_recv()
    to_all(fx, frecv, 1)
    for copy in y_in[1:] + halos + mates:
        copy.wait_recv()
    own_a.wait()


    def block(xb, carry):
        keep = jnp.where(yl * 32 + xb * 8 + z == 0, 0.0, 1.0).astype(F32)
        a = abuf[xb]
        filtered = []
        for j in range(3):
            wj = wbuf[j].reshape(D, CQ)
            bs[j] = jnp.dot(a, wj, preferred_element_type=F32).astype(BF).astype(F32)
            bs[j, pl.ds(0, HALO)] = bs[j, pl.ds(0, HALO)] * keep
            lanes = pl.ds(pl.multiple_of(x * CQ, CQ), CQ)
            total = taps[j, pl.ds(0, 1), lanes] * bs[j, pl.ds(HALO, BLK)]
            for k in range(1, TAPS):
                total = total + taps[j, pl.ds(k, 1), lanes] * bs[j, pl.ds(HALO - k, BLK)]
            filtered.append(total)
        drv[:, xb] = (filtered[0] * filtered[2]).T.astype(BF).reshape(16, 16, BLK)
        spread(lambda p: drv.at[p, xb], drecv.at[me, xb], 0)
        qry[xb] = filtered[1].T.astype(BF)
        return carry

    lax.fori_loop(0, NX, block, 0)
    pltpu.make_async_copy(drv.at[me], drecv.at[me], own_sem.at[0]).start()
    own_q = pltpu.make_async_copy(qry.at[x], qrecv.at[x], local_sem.at[0])
    own_q.start()
    q_in = [go.start(qry.at[xp], qrecv.at[x], to) for xp, to in ((xr, to_xr), (xl, to_xl), (xo, to_xo))]

    def inner(value):
        high, low = split(value)
        return (
            jnp.dot(high, wide_h[...], preferred_element_type=F32)
            + jnp.dot(low, wide_h[...], preferred_element_type=F32)
            + jnp.dot(high, wide_l[...], preferred_element_type=F32)
        )

    def widen(source):
        for side in range(2):
            half = source[:, :, :, 128 * side : 128 * side + 128]
            wide[side] = half.astype(F32).reshape(1024, 128)

    def spectrum(first):
        parts = []
        for i in range(GROUP):
            rows = jnp.concatenate(
                [wide[side, pl.ds(first + i, 64, stride=16), :] for side in range(2)], axis=1
            ).astype(BF)
            both = jnp.dot(ahead[...], jnp.concatenate([rows, rows], axis=0), preferred_element_type=F32)
            re, im = both[:64], both[64:]
            parts.append(
                jnp.concatenate([re * turn[0] - im * turn[1], re * turn[1] + im * turn[0]], axis=1)
            )
        return inner(jnp.concatenate(parts, axis=0))

    def filter_group(g, carry):
        spec[g] = spectrum(g * GROUP)
        return carry

    def signal_group(g, carry):
        first = g * GROUP
        s = spectrum(first)
        sr, si, hr, hi = s[:, :BLK], s[:, BLK:], spec[g, :, :BLK], spec[g, :, BLK:]
        v = inner(jnp.concatenate([sr * hr - si * hi, -(sr * hi + si * hr)], axis=1))
        for i in range(GROUP):
            re, im = v[64 * i : 64 * i + 64, :BLK], -v[64 * i : 64 * i + 64, BLK:]
            both = jnp.concatenate([re * turn[0] + im * turn[1], im * turn[0] - re * turn[1]], axis=0)
            high, low = split(both)
            y = jnp.dot(back[...], jnp.concatenate([high, low, high], axis=0), preferred_element_type=F32)
            for side in range(2):
                out32[side, pl.ds(first + i, 64, stride=16), :] = y[:, 128 * side : 128 * side + 128]
        return carry

    await_all(fx, frecv, 1)
    widen(frecv)
    lax.fori_loop(0, 16 // GROUP, filter_group, 0)
    await_all(drv, drecv, 0)
    widen(drecv)
    lax.fori_loop(0, 16 // GROUP, signal_group, 0)
    for side in range(2):
        osend[:, :, 128 * side : 128 * side + 128] = out32[side].reshape(64, 16, 128).astype(BF)

    slot = x * 16 + me

    def home(t, carry):
        c = lax.rem(ctx + t, 64)
        yt, xt, zt = lax.div(c, 32), lax.rem(lax.div(c, 8), 4), lax.rem(c, 8)
        pltpu.make_async_remote_copy(
            src_ref=osend.at[(yt * NZ + zt) * NX + xt],
            dst_ref=crecv.at[slot],
            send_sem=all_send.at[2],
            recv_sem=all_recv.at[2],
            device_id={"ctx": c},
            device_id_type=MESH,
        ).start()
        return carry

    lax.fori_loop(1, 64, home, 0)
    own_c = pltpu.make_async_copy(osend.at[me * NX + x], crecv.at[slot], own_sem.at[2])
    own_c.start()
    own_q.wait()
    for copy in q_in:
        copy.wait_recv()
    for copy in own_o:
        copy.wait()
    own_c.wait()
    pltpu.make_async_copy(crecv.at[pl.ds(0, 63)], crecv.at[pl.ds(0, 63)], all_recv.at[2]).wait()
    gated = (qrecv[...].reshape(1024, BLK).astype(F32) * crecv[...].reshape(1024, BLK).astype(F32)).astype(BF)
    gated = gated.T

    def partial(h):
        return jnp.dot(gated, obuf[h], preferred_element_type=F32)

    far_h, near_h = (1 - yh) * 2, yh * 2
    psend[0] = partial(far_h + 1 - core).astype(BF)
    p_in = [go.start(psend.at[0], precv.at[0], mate)]
    total = partial(far_h + core)
    p_in[0].wait_recv()
    ysend[...] = (total + precv[0].astype(F32)).astype(BF)
    y_copy = go.start(ysend, yrecv, across)
    psend[1] = partial(near_h + 1 - core).astype(BF)
    p_in.append(go.start(psend.at[1], precv.at[1], mate))
    total = partial(near_h + core)
    p_in[1].wait_recv()
    total = total + precv[1].astype(F32)
    y_copy.wait_recv()
    out[...] = (total + yrecv[...].astype(F32)).astype(BF)

    go.wait_sends()
    sent_all(drv, 0)
    sent_all(fx, 1)
    sent_all(osend, 2, 63)


def layer(act, w, taps, flt, w_out):
    any_space, vmem = pl.BlockSpec(memory_space=pl.ANY), pl.BlockSpec(memory_space=pltpu.VMEM)
    return pl.pallas_call(
        layer_kernel,
        out_shape=jax.ShapeDtypeStruct((BLK, 1024), BF),
        in_specs=[any_space, any_space, vmem, any_space, any_space] + [vmem] * 5,
        out_specs=vmem,
        scratch_shapes=[
            pltpu.VMEM((NX, ROWS, D), BF),
            pltpu.VMEM((3, NY, NX, NZ, DB, CQ), BF),
            pltpu.VMEM((3, ROWS, CQ), F32),
            pltpu.VMEM((1024, BLK), F32),
            pltpu.VMEM((NX, 16, 16, BLK), BF),
            pltpu.VMEM((16, NX, 16, BLK), BF),
            pltpu.VMEM((16, NX, 16, BLK), BF),
            pltpu.VMEM((16, NX, 16, BLK), BF),
            pltpu.VMEM((16, NX, 16, BLK), BF),
            pltpu.VMEM((NX, CQ, BLK), BF),
            pltpu.VMEM((NX, CQ, BLK), BF),
            pltpu.VMEM((2, 1024, 128), F32),
            pltpu.VMEM((2, 1024, 128), F32),
            pltpu.VMEM((16 // GROUP, 64 * GROUP, 2 * BLK), F32),
            pltpu.VMEM((64, 16, BLK), BF),
            pltpu.VMEM((64, 16, BLK), BF),
            pltpu.VMEM((4, 1024, 1024), BF),
            pltpu.VMEM((2, BLK, 1024), BF),
            pltpu.VMEM((2, BLK, 1024), BF),
            pltpu.VMEM((BLK, 1024), BF),
            pltpu.VMEM((BLK, 1024), BF),
            pltpu.SemaphoreType.DMA((8,)),
            pltpu.SemaphoreType.DMA((3,)),
            pltpu.SemaphoreType.DMA((3,)),
            pltpu.SemaphoreType.DMA((3,)),
            pltpu.SemaphoreType.DMA((N_COPIES,)),
            pltpu.SemaphoreType.DMA((N_COPIES,)),
        ],
        compiler_params=pltpu.CompilerParams(
            collective_id=0, has_side_effects=True, vmem_limit_bytes=58 * 1024 * 1024
        ),
        name="layer",
    )(act, w, taps, flt, w_out, *[jnp.asarray(table) for table in tables()])


def on_device(activations, w_in, short_taps, long_filter, w_out):
    return layer(activations, w_in, short_taps.transpose(0, 2, 1), long_filter, w_out)


def solution(mesh):
    return jax.shard_map(
        on_device,
        mesh=mesh,
        in_specs=(
            P("ctx", None),
            P(None, "ctx", "hid"),
            P(None, "hid", None),
            P("hid", "ctx"),
            P("hid", None),
        ),
        out_specs=P("ctx", "hid"),
        check_vma=False,
    )
```

```python
import math

import numpy as np
import ml_dtypes
import jax
import jax.numpy as jnp
from jax import lax
from jax.experimental import pallas as pl
from jax.experimental.pallas import tpu as pltpu
from jax.sharding import PartitionSpec as P

MESH = pl.DeviceIdType.MESH
BF = jnp.bfloat16
F32 = jnp.float32
TAPS = 3
NY, NX, NZ = 2, 4, 8
BLK = 256
HALO = 16
ROWS = BLK + HALO
D = 4096
CQ = 256
DB = 64


def place():
    ctx = lax.axis_index("ctx")
    hid = lax.axis_index("hid")
    yl = lax.div(ctx, 32)
    x = lax.rem(lax.div(ctx, 8), 4)
    z = lax.rem(ctx, 8)
    return ctx, hid, yl, x, z


def at_ctx(yl, x, z):
    return {"ctx": yl * 32 + x * 8 + z}


class Copies:
    def __init__(self, send, recv):
        self.send, self.recv, self.all = send, recv, []

    def start(self, src, dst, device):
        k = len(self.all)
        copy = pltpu.make_async_remote_copy(
            src_ref=src,
            dst_ref=dst,
            send_sem=self.send.at[k],
            recv_sem=self.recv.at[k],
            device_id=device,
            device_id_type=MESH,
        )
        copy.start()
        self.all.append(copy)
        return copy

    def wait_sends(self):
        for copy in self.all:
            copy.wait_send()


def halves(table):
    high = table.astype(ml_dtypes.bfloat16)
    low = (table - high.astype(np.float64)).astype(ml_dtypes.bfloat16)
    return high, low


def tables():
    order = np.array([yl * 32 + x * 8 + z for yl in range(NY) for z in range(NZ) for x in range(NX)])
    k1 = np.arange(64) + 0.5
    angle = 2 * np.pi * np.outer(k1, np.arange(64)) / 128
    ahead = np.concatenate([np.cos(angle), -np.sin(angle)], axis=0)
    back = np.concatenate([np.cos(angle.T), -np.sin(angle.T)], axis=1) * 2.0**-14
    turn = 2 * np.pi * np.outer(k1, np.arange(BLK)) / 32768
    inner = 2 * np.pi * (np.outer(np.arange(BLK), np.arange(BLK)) % BLK) / BLK
    c, s = np.cos(inner), np.sin(inner)
    wide = np.block([[c, -s], [s, c]])
    sides = np.array([part * BLK + side * 128 + i for side in range(2) for part in range(2) for i in range(128)])
    wide = wide[sides][:, sides]
    ahead_h, ahead_l = halves(ahead[:, order])
    back_h, back_l = halves(back[order])
    wide_h, wide_l = halves(wide)
    return (
        np.concatenate([ahead_h, ahead_l], axis=1),
        np.stack([np.cos(turn), -np.sin(turn)]).astype(np.float32),
        wide_h,
        wide_l,
        np.concatenate([back_h, back_h, back_l], axis=1),
    )


N_COPIES = 120
UNITS = {"b0": (0, 0, 3), "b1": (1, 0, 3), "b2": (3, 2, 1), "a0": (2, 0, 3), "a1": (3, 0, 2)}
GROUP = 4


def split(value):
    high = value.astype(BF)
    return high, (value - high.astype(F32)).astype(BF)


def layer_kernel(
    act, w, taps, flt, w_out, ahead, turn, wide_h, wide_l, back, out,
    abuf, wbuf, bs, f32buf, f16buf, fx, frecv, drv, drecv, qry, qrecv, wide, out32, spec, p_high, p_low, osend, crecv,
    obuf, psend, precv, ysend, yrecv, held, local_sem, own_sem, all_send, all_recv, send_sem, recv_sem,
):
    ctx, hid, yl, x, z = place()
    core = lax.rem(hid, 2)
    yh = lax.div(hid, 2)
    mate = {"hid": hid + 1 - 2 * core}
    across = {"hid": lax.rem(hid + 2, 4)}
    me = yl * NZ + z
    right, left = lax.rem(z + 1, NZ), lax.rem(z + NZ - 1, NZ)
    xr, xl, xo = lax.rem(x + 1, NX), lax.rem(x + 3, NX), lax.rem(x + 2, NX)
    after = lax.rem(ctx + 1, 64)
    to_r, to_l = at_ctx(yl, x, right), at_ctx(yl, x, left)
    to_y = at_ctx(1 - yl, x, z)
    to_xr, to_xl, to_xo = at_ctx(yl, xr, z), at_ctx(yl, xl, z), at_ctx(yl, xo, z)

    own_w = pltpu.make_async_copy(
        w.at[:, :, pl.ds(pl.multiple_of(x * CQ, CQ), CQ)], wbuf.at[:, yl, x, z], local_sem.at[0]
    )
    own_a = pltpu.make_async_copy(act, abuf.at[x, pl.ds(HALO, BLK)], local_sem.at[1])
    own_w.start()
    own_a.start()

    own_f = pltpu.make_async_copy(flt, f32buf, local_sem.at[2])
    own_f.start()
    own_o = [
        pltpu.make_async_copy(w_out.at[:, pl.ds(1024 * h, 1024)], obuf.at[h], local_sem.at[3 + h])
        for h in range(4)
    ]
    for copy in own_o:
        copy.start()

    own_f.wait()
    f16buf[...] = f32buf[...].astype(BF).reshape(NX, 16, 16, BLK)
    own_x = pltpu.make_async_copy(f16buf.at[x], fx.at[:, x], local_sem.at[2])
    own_x.start()
    barrier = pltpu.get_barrier_semaphore()

    def greet(t, carry):
        pl.semaphore_signal(barrier, inc=1, device_id={"ctx": lax.rem(ctx + t, 64)}, device_id_type=MESH)
        return carry

    lax.fori_loop(1, 64, greet, 0)
    for peer in (mate, across):
        pl.semaphore_signal(barrier, inc=1, device_id=peer, device_id_type=MESH)
    pl.semaphore_wait(barrier, 65)

    go = Copies(send_sem, recv_sem)

    def spread(src, dst, sem):
        def one(t, carry):
            p = lax.rem(me + t, 16)
            pltpu.make_async_remote_copy(
                src_ref=src(p),
                dst_ref=dst,
                send_sem=all_send.at[sem],
                recv_sem=all_recv.at[sem],
                device_id=at_ctx(lax.div(p, NZ), x, lax.rem(p, NZ)),
                device_id_type=MESH,
            ).start()
            return carry

        lax.fori_loop(1, 16, one, 0)

    def to_all(src, dst, sem):
        spread(lambda p: src.at[p], dst.at[me], sem)
        pltpu.make_async_copy(src.at[me], dst.at[me], own_sem.at[sem]).start()

    def await_all(src, dst, sem):
        pltpu.make_async_copy(src.at[me], dst.at[me], own_sem.at[sem]).wait()
        pltpu.make_async_copy(dst.at[pl.ds(0, 15)], dst.at[pl.ds(0, 15)], all_recv.at[sem]).wait()

    def sent_all(src, sem, count=15):
        pltpu.make_async_copy(src.at[pl.ds(0, count)], src.at[pl.ds(0, count)], all_send.at[sem]).wait()

    first = []
    for xp, to in ((xr, to_xr), (xl, to_xl), (xo, to_xo)):
        first.append(
            go.start(w.at[:, :, pl.ds(pl.multiple_of(xp * CQ, CQ), CQ)], wbuf.at[:, yl, x, z], to)
        )

    def unit(name, zs):
        ys = 1 - yl if name[0] == "p" else yl
        xs, j, count = UNITS[name.replace("p", "a")]
        return wbuf.at[pl.ds(j, count), ys, lax.rem(x + xs, NX), zs]

    def send(name, zs, to):
        part = unit(name, zs)
        return go.start(part, part, to)

    from_l, from_r, y_in = {}, {}, {}

    def send_own(name):
        from_l[name, 1] = send(name, z, to_r)
        from_r[name, 1] = send(name, z, to_l)

    own_w.wait()
    send_own("b0")
    y_in["b0"] = send("b0", z, to_y)
    x_next = lax.rem(lax.div(after, 8), 4)
    lanes = pl.ds(pl.multiple_of(core * (D // 2), D // 2), D // 2)
    halo_in = go.start(
        act.at[pl.ds(BLK - HALO, HALO), lanes], abuf.at[x_next, pl.ds(0, HALO), lanes], {"ctx": after}
    )
    first[1].wait_recv()
    send_own("b1")
    y_in["b1"] = send("b1", z, to_y)
    first[0].wait_recv()
    y_in["a1"] = send("a1", z, to_y)
    send_own("b2")
    y_in["b2"] = send("b2", z, to_y)
    first[2].wait_recv()
    y_in["a0"] = send("a0", z, to_y)
    send_own("a1")
    send_own("a0")

    def a_rows(part):
        return pl.multiple_of(core * 128 + part * 64, 64)

    def a_slot(block, part, count=64):
        return abuf.at[block, pl.ds(pl.multiple_of(HALO + core * 128 + part * 64, 16), count)]

    def a_send(part, to):
        return go.start(act.at[pl.ds(a_rows(part), 64)], a_slot(x, part), to)

    near = [a_send(0, to_xr), a_send(1, to_xl)]
    fx_in = [go.start(f16buf.at[xp], fx.at[:, x], to) for xp, to in ((xr, to_xr), (xl, to_xl), (xo, to_xo))]
    for name in ("a1", "a0"):
        y_in[name].wait_recv()
        send_own(name.replace("a", "p"))

    def relay(step):
        zl, zr = lax.rem(z + NZ - step, NZ), lax.rem(z + step, NZ)
        for name in ("b0", "b1", "b2", "a1", "a0", "p1", "p0"):
            for source, zs, to, last in ((from_l, zl, to_r, ("b0", "a1", "a0")), (from_r, zr, to_l, ("b1", "b2", "p1", "p0"))):
                source[name, step].wait_recv()
                if step < 3 or name in last:
                    source[name, step + 1] = send(name, zs, to)
                if name[0] == "b":
                    y_in[name, step, to is to_r] = send(name, zs, to_y)

    relay(1)
    near += [a_send(1, to_xr), a_send(0, to_xl)]
    near[0].wait_recv()
    far = [go.start(a_slot(xl, 0), a_slot(xl, 0), to_xr)]
    near[1].wait_recv()
    far.append(go.start(a_slot(xr, 1), a_slot(xr, 1), to_xl))
    halo_in.wait_recv()
    halo_own = abuf.at[x, pl.ds(0, HALO), lanes]
    halos = [go.start(halo_own, halo_own, to) for to in (to_xr, to_xl, to_xo)]
    mates = [go.start(a_slot(xl, 0), a_slot(xl, 0), mate), go.start(a_slot(xr, 1), a_slot(xr, 1), mate)]
    relay(2)
    for copy in halos:
        copy.wait_recv()
    halo_all = abuf.at[:, pl.ds(0, HALO), lanes]
    mates.append(go.start(halo_all, halo_all, mate))
    relay(3)
    for copy, block, part in ((near[2], xl, 1), (near[3], xr, 0), (far[0], xo, 0), (far[1], xo, 1)):
        copy.wait_recv()
        mates.append(go.start(a_slot(block, part), a_slot(block, part), mate))
    zo = lax.rem(z + 4, NZ)
    for name in ("b0", "b1", "b2", "a1", "p1", "a0", "p0"):
        (from_l if name in ("b0", "a1", "a0") else from_r)[name, 4].wait_recv()
        if name[0] == "b":
            y_in[name, 4] = send(name, zo, to_y)
    own_x.wait()
    for copy in fx_in:
        copy.wait_recv()
    to_all(fx, frecv, 1)
    for name, copy in y_in.items():
        if name not in ("a0", "a1"):
            copy.wait_recv()
    for copy in mates:
        copy.wait_recv()
    own_a.wait()

    def block(xb, carry):
        keep = jnp.where(yl * 32 + xb * 8 + z == 0, 0.0, 1.0).astype(F32)
        a = abuf[xb]
        filtered = []
        for j in range(3):
            wj = wbuf[j].reshape(D, CQ)
            bs[j] = jnp.dot(a, wj, preferred_element_type=F32).astype(BF).astype(F32)
            bs[j, pl.ds(0, HALO)] = bs[j, pl.ds(0, HALO)] * keep
            mine = pl.ds(pl.multiple_of(x * CQ, CQ), CQ)
            total = taps[j, pl.ds(0, 1), mine] * bs[j, pl.ds(HALO, BLK)]
            for k in range(1, TAPS):
                total = total + taps[j, pl.ds(k, 1), mine] * bs[j, pl.ds(HALO - k, BLK)]
            filtered.append(total)
        drv[:, xb] = (filtered[0] * filtered[2]).T.astype(BF).reshape(16, 16, BLK)
        spread(lambda p: drv.at[p, xb], drecv.at[me, xb], 0)
        qry[xb] = filtered[1].T.astype(BF)
        return carry

    lax.fori_loop(0, NX, block, 0)
    pltpu.make_async_copy(drv.at[me], drecv.at[me], own_sem.at[0]).start()
    own_q = pltpu.make_async_copy(qry.at[x], qrecv.at[x], local_sem.at[0])
    own_q.start()
    q_in = [go.start(qry.at[xp], qrecv.at[x], to) for xp, to in ((xr, to_xr), (xl, to_xl), (xo, to_xo))]

    def inner(high, low, columns):
        return (
            jnp.dot(high, wide_h[:, columns], preferred_element_type=F32)
            + jnp.dot(low, wide_h[:, columns], preferred_element_type=F32)
            + jnp.dot(high, wide_l[:, columns], preferred_element_type=F32)
        )

    def widen(source):
        for side in range(2):
            half = source[:, :, :, 128 * side : 128 * side + 128]
            wide[side] = half.astype(F32).reshape(1024, 128)

    def spectrum(first):
        parts = []
        for i in range(GROUP):
            rows = jnp.concatenate(
                [wide[side, pl.ds(first + i, 64, stride=16), :] for side in range(2)], axis=1
            ).astype(BF)
            both = jnp.dot(ahead[...], jnp.concatenate([rows, rows], axis=0), preferred_element_type=F32)
            pieces = []
            for side in range(2):
                at = slice(128 * side, 128 * side + 128)
                re, im, tr, ti = both[:64, at], both[64:, at], turn[0, :, at], turn[1, :, at]
                pieces += [re * tr - im * ti, re * ti + im * tr]
            parts.append(jnp.concatenate(pieces, axis=1))
        return inner(*split(jnp.concatenate(parts, axis=0)), slice(None))

    def filter_group(g, carry):
        spec[g] = spectrum(g * GROUP)
        return carry

    def signal_group(g, carry):
        s = spectrum(g * GROUP)
        for side in range(2):
            re, im = slice(256 * side, 256 * side + 128), slice(256 * side + 128, 256 * side + 256)
            sr, si, hr, hi = s[:, re], s[:, im], spec[g, :, re], spec[g, :, im]
            p_high[g, :, re], p_low[g, :, re] = split(sr * hr - si * hi)
            p_high[g, :, im], p_low[g, :, im] = split(-(sr * hi + si * hr))
        return carry

    def inverse_group(side):
        at = slice(128 * side, 128 * side + 128)

        def one(g, carry):
            v = inner(p_high[g], p_low[g], slice(256 * side, 256 * side + 256))
            for i in range(0, GROUP, 2):
                pair = []
                for c in (i, i + 1):
                    re, im = v[64 * c : 64 * c + 64, :128], -v[64 * c : 64 * c + 64, 128:]
                    tr, ti = turn[0, :, at], turn[1, :, at]
                    pair.append(jnp.concatenate([re * tr + im * ti, im * tr - re * ti], axis=0))
                high, low = split(jnp.concatenate(pair, axis=1))
                y = jnp.dot(back[...], jnp.concatenate([high, low, high], axis=0), preferred_element_type=F32)
                out32[side, pl.ds(g * GROUP + i, 64, stride=16), :] = y[:, :128]
                out32[side, pl.ds(g * GROUP + i + 1, 64, stride=16), :] = y[:, 128:]
            return carry

        return one

    await_all(fx, frecv, 1)
    widen(frecv)
    lax.fori_loop(0, 16 // GROUP, filter_group, 0)
    await_all(drv, drecv, 0)
    widen(drecv)
    lax.fori_loop(0, 16 // GROUP, signal_group, 0)

    slot = x * 16 + me
    own_c = []
    for side in range(2):
        lax.fori_loop(0, 16 // GROUP, inverse_group(side), 0)
        osend[side] = out32[side].reshape(64, 16, 128).astype(BF)

        def home(t, carry):
            c = lax.rem(ctx + t, 64)
            yt, xt, zt = lax.div(c, 32), lax.rem(lax.div(c, 8), 4), lax.rem(c, 8)
            pltpu.make_async_remote_copy(
                src_ref=osend.at[side, (yt * NZ + zt) * NX + xt],
                dst_ref=crecv.at[side, slot],
                send_sem=all_send.at[2 + side],
                recv_sem=all_recv.at[2 + side],
                device_id={"ctx": c},
                device_id_type=MESH,
            ).start()
            return carry

        lax.fori_loop(1, 64, home, 0)
        own_c.append(
            pltpu.make_async_copy(osend.at[side, me * NX + x], crecv.at[side, slot], own_sem.at[2 + side])
        )
        own_c[side].start()

    own_q.wait()
    for copy in q_in:
        copy.wait_recv()
    for copy in own_o:
        copy.wait()

    far_h, near_h = (1 - yh) * 2, yh * 2
    p_in, y_copy = {}, []
    for side in range(2):
        own_c[side].wait()
        arrived = crecv.at[side, pl.ds(0, 63)]
        pltpu.make_async_copy(arrived, arrived, all_recv.at[2 + side]).wait()
        query = qrecv[:, :, 128 * side : 128 * side + 128].reshape(1024, 128).astype(F32)
        gated = (query * crecv[side].reshape(1024, 128).astype(F32)).T.astype(BF)

        def partial(h):
            return jnp.dot(gated, obuf[h], preferred_element_type=F32)

        psend[side, 0] = partial(far_h + 1 - core).astype(BF)
        p_in[side, 0] = go.start(psend.at[side, 0], precv.at[side, 0], mate)
        total = partial(far_h + core)
        p_in[side, 0].wait_recv()
        ysend[side] = (total + precv[side, 0].astype(F32)).astype(BF)
        y_copy.append(go.start(ysend.at[side], yrecv.at[side], across))
        psend[side, 1] = partial(near_h + 1 - core).astype(BF)
        p_in[side, 1] = go.start(psend.at[side, 1], precv.at[side, 1], mate)
        held[side] = partial(near_h + core)
    for side in range(2):
        p_in[side, 1].wait_recv()
        y_copy[side].wait_recv()
        total = held[side] + precv[side, 1].astype(F32) + yrecv[side].astype(F32)
        out[pl.ds(128 * side, 128), :] = total.astype(BF)

    go.wait_sends()
    sent_all(drv, 0)
    sent_all(fx, 1)
    for side in range(2):
        sent_all(osend.at[side], 2 + side, 63)


def layer(act, w, taps, flt, w_out):
    any_space, vmem = pl.BlockSpec(memory_space=pl.ANY), pl.BlockSpec(memory_space=pltpu.VMEM)
    return pl.pallas_call(
        layer_kernel,
        out_shape=jax.ShapeDtypeStruct((BLK, 1024), BF),
        in_specs=[any_space, any_space, vmem, any_space, any_space] + [vmem] * 5,
        out_specs=vmem,
        scratch_shapes=[
            pltpu.VMEM((NX, ROWS, D), BF),
            pltpu.VMEM((3, NY, NX, NZ, DB, CQ), BF),
            pltpu.VMEM((3, ROWS, CQ), F32),
            pltpu.VMEM((1024, BLK), F32),
            pltpu.VMEM((NX, 16, 16, BLK), BF),
            pltpu.VMEM((16, NX, 16, BLK), BF),
            pltpu.VMEM((16, NX, 16, BLK), BF),
            pltpu.VMEM((16, NX, 16, BLK), BF),
            pltpu.VMEM((16, NX, 16, BLK), BF),
            pltpu.VMEM((NX, CQ, BLK), BF),
            pltpu.VMEM((NX, CQ, BLK), BF),
            pltpu.VMEM((2, 1024, 128), F32),
            pltpu.VMEM((2, 1024, 128), F32),
            pltpu.VMEM((16 // GROUP, 64 * GROUP, 2 * BLK), F32),
            pltpu.VMEM((16 // GROUP, 64 * GROUP, 2 * BLK), BF),
            pltpu.VMEM((16 // GROUP, 64 * GROUP, 2 * BLK), BF),
            pltpu.VMEM((2, 64, 16, 128), BF),
            pltpu.VMEM((2, 64, 16, 128), BF),
            pltpu.VMEM((4, 1024, 1024), BF),
            pltpu.VMEM((2, 2, 128, 1024), BF),
            pltpu.VMEM((2, 2, 128, 1024), BF),
            pltpu.VMEM((2, 128, 1024), BF),
            pltpu.VMEM((2, 128, 1024), BF),
            pltpu.VMEM((2, 128, 1024), F32),
            pltpu.SemaphoreType.DMA((8,)),
            pltpu.SemaphoreType.DMA((4,)),
            pltpu.SemaphoreType.DMA((4,)),
            pltpu.SemaphoreType.DMA((4,)),
            pltpu.SemaphoreType.DMA((N_COPIES,)),
            pltpu.SemaphoreType.DMA((N_COPIES,)),
        ],
        compiler_params=pltpu.CompilerParams(
            collective_id=0, has_side_effects=True, vmem_limit_bytes=58 * 1024 * 1024
        ),
        name="layer",
    )(act, w, taps, flt, w_out, *[jnp.asarray(table) for table in tables()])


def on_device(activations, w_in, short_taps, long_filter, w_out):
    return layer(activations, w_in, short_taps.transpose(0, 2, 1), long_filter, w_out)


def solution(mesh):
    return jax.shard_map(
        on_device,
        mesh=mesh,
        in_specs=(
            P("ctx", None),
            P(None, "ctx", "hid"),
            P(None, "hid", None),
            P("hid", "ctx"),
            P("hid", None),
        ),
        out_specs=P("ctx", "hid"),
        check_vma=False,
    )
```

```python
import math

import numpy as np
import ml_dtypes
import jax
import jax.numpy as jnp
from jax import lax
from jax.experimental import pallas as pl
from jax.experimental.pallas import tpu as pltpu
from jax.sharding import PartitionSpec as P

MESH = pl.DeviceIdType.MESH
BF = jnp.bfloat16
F32 = jnp.float32
TAPS = 3
NY, NX, NZ = 2, 4, 8
BLK = 256
HALO = 16
ROWS = BLK + HALO
D = 4096
CQ = 256
DB = 64


def place():
    ctx = lax.axis_index("ctx")
    hid = lax.axis_index("hid")
    yl = lax.div(ctx, 32)
    x = lax.rem(lax.div(ctx, 8), 4)
    z = lax.rem(ctx, 8)
    return ctx, hid, yl, x, z


def at_ctx(yl, x, z):
    return {"ctx": yl * 32 + x * 8 + z}


class Copies:
    def __init__(self, send, recv):
        self.send, self.recv, self.all = send, recv, []

    def start(self, src, dst, device):
        k = len(self.all)
        copy = pltpu.make_async_remote_copy(
            src_ref=src,
            dst_ref=dst,
            send_sem=self.send.at[k],
            recv_sem=self.recv.at[k],
            device_id=device,
            device_id_type=MESH,
        )
        copy.start()
        self.all.append(copy)
        return copy

    def wait_sends(self):
        for copy in self.all:
            copy.wait_send()


def halves(table):
    high = table.astype(ml_dtypes.bfloat16)
    low = (table - high.astype(np.float64)).astype(ml_dtypes.bfloat16)
    return high, low


def tables():
    order = np.array([yl * 32 + x * 8 + z for yl in range(NY) for z in range(NZ) for x in range(NX)])
    k1 = np.arange(64) + 0.5
    angle = 2 * np.pi * np.outer(k1, np.arange(64)) / 128
    ahead = np.concatenate([np.cos(angle), -np.sin(angle)], axis=0)
    back = np.concatenate([np.cos(angle.T), -np.sin(angle.T)], axis=1) * 2.0**-14
    turn = 2 * np.pi * np.outer(k1, np.arange(BLK)) / 32768
    inner = 2 * np.pi * (np.outer(np.arange(BLK), np.arange(BLK)) % BLK) / BLK
    c, s = np.cos(inner), np.sin(inner)
    wide = np.block([[c, -s], [s, c]])
    sides = np.array([part * BLK + side * 128 + i for side in range(2) for part in range(2) for i in range(128)])
    wide = wide[sides][:, sides]
    ahead_h, ahead_l = halves(ahead[:, order])
    back_h, back_l = halves(back[order])
    wide_h, wide_l = halves(wide)
    return (
        np.concatenate([ahead_h, ahead_l], axis=1),
        np.stack([np.cos(turn), -np.sin(turn)]).astype(np.float32),
        wide_h,
        wide_l,
        np.concatenate([back_h, back_h, back_l], axis=1),
    )


N_COPIES = 120
UNITS = {"b0": (0, 0, 3), "b1": (1, 0, 3), "b2": (3, 2, 1), "a0": (2, 0, 3), "a1": (3, 0, 2)}
GROUP = 4


def split(value):
    high = value.astype(BF)
    return high, (value - high.astype(F32)).astype(BF)


def layer_kernel(
    act, w, taps_in, flt, w_out, ahead_in, turn_in, wide_h_in, wide_l_in, back_in, out,
    taps, ahead, turn, wide_h, wide_l, back, abuf, wbuf, bs, f32buf, f16buf, frecv, drv, drecv, qry, qrecv, wide, out32, spec, p_high, p_low, osend, crecv,
    obuf, psend, precv, ysend, yrecv, held, local_sem, own_sem, all_send, all_recv, send_sem, recv_sem,
):
    tables_here = (
        (taps_in, taps), (ahead_in, ahead), (turn_in, turn), (wide_h_in, wide_h), (wide_l_in, wide_l), (back_in, back)
    )
    ctx, hid, yl, x, z = place()
    core = lax.rem(hid, 2)
    yh = lax.div(hid, 2)
    mate = {"hid": hid + 1 - 2 * core}
    across = {"hid": lax.rem(hid + 2, 4)}
    me = yl * NZ + z
    right, left = lax.rem(z + 1, NZ), lax.rem(z + NZ - 1, NZ)
    xr, xl, xo = lax.rem(x + 1, NX), lax.rem(x + 3, NX), lax.rem(x + 2, NX)
    after, before = lax.rem(ctx + 1, 64), lax.rem(ctx + 63, 64)
    to_r, to_l = at_ctx(yl, x, right), at_ctx(yl, x, left)
    to_y = at_ctx(1 - yl, x, z)
    to_xr, to_xl, to_xo = at_ctx(yl, xr, z), at_ctx(yl, xl, z), at_ctx(yl, xo, z)

    own_w = pltpu.make_async_copy(
        w.at[:, :, pl.ds(pl.multiple_of(x * CQ, CQ), CQ)], wbuf.at[:, yl, x, z], local_sem.at[0]
    )
    own_a = pltpu.make_async_copy(act, abuf.at[x, pl.ds(HALO, BLK)], local_sem.at[1])
    own_w.start()
    own_a.start()

    barrier = pltpu.get_barrier_semaphore()
    for peer in (to_xr, to_xl, to_xo, to_r, to_l, to_y, mate, across, {"ctx": after}, {"ctx": before}):
        pl.semaphore_signal(barrier, inc=1, device_id=peer, device_id_type=MESH)
    pl.semaphore_wait(barrier, 10)

    go = Copies(send_sem, recv_sem)

    def spread(src, dst, sem):
        def one(t, carry):
            p = lax.rem(me + t, 16)
            pltpu.make_async_remote_copy(
                src_ref=src(p),
                dst_ref=dst,
                send_sem=all_send.at[sem],
                recv_sem=all_recv.at[sem],
                device_id=at_ctx(lax.div(p, NZ), x, lax.rem(p, NZ)),
                device_id_type=MESH,
            ).start()
            return carry

        lax.fori_loop(1, 16, one, 0)

    first = []
    for xp, to in ((xr, to_xr), (xl, to_xl), (xo, to_xo)):
        first.append(
            go.start(w.at[:, :, pl.ds(pl.multiple_of(xp * CQ, CQ), CQ)], wbuf.at[:, yl, x, z], to)
        )

    def unit(name, zs):
        ys = 1 - yl if name[0] == "p" else yl
        xs, j, count = UNITS[name.replace("p", "a")]
        return wbuf.at[pl.ds(j, count), ys, lax.rem(x + xs, NX), zs]

    def send(name, zs, to):
        part = unit(name, zs)
        return go.start(part, part, to)

    from_l, from_r, y_in = {}, {}, {}

    def send_own(name):
        from_l[name, 1] = send(name, z, to_r)
        from_r[name, 1] = send(name, z, to_l)

    own_w.wait()
    send_own("b0")
    y_in["b0"] = send("b0", z, to_y)
    x_next = lax.rem(lax.div(after, 8), 4)
    lanes = pl.ds(pl.multiple_of(core * (D // 2), D // 2), D // 2)
    halo_in = go.start(
        act.at[pl.ds(BLK - HALO, HALO), lanes], abuf.at[x_next, pl.ds(0, HALO), lanes], {"ctx": after}
    )
    first[1].wait_recv()
    send_own("b1")
    y_in["b1"] = send("b1", z, to_y)
    first[0].wait_recv()
    y_in["a1"] = send("a1", z, to_y)
    send_own("b2")
    y_in["b2"] = send("b2", z, to_y)
    first[2].wait_recv()
    y_in["a0"] = send("a0", z, to_y)
    send_own("a1")
    send_own("a0")

    def a_rows(part):
        return pl.multiple_of(core * 128 + part * 64, 64)

    def a_slot(block, part, count=64):
        return abuf.at[block, pl.ds(pl.multiple_of(HALO + core * 128 + part * 64, 16), count)]

    def a_send(part, to):
        return go.start(act.at[pl.ds(a_rows(part), 64)], a_slot(x, part), to)

    near = [a_send(0, to_xr), a_send(1, to_xl)]
    loads = [pltpu.make_async_copy(flt, f32buf, local_sem.at[2])]
    for k, (table, kept) in enumerate(tables_here):
        loads.append(pltpu.make_async_copy(table, kept, local_sem.at[7 + k]))
    own_o = [
        pltpu.make_async_copy(w_out.at[:, pl.ds(1024 * h, 1024)], obuf.at[h], local_sem.at[3 + h])
        for h in range(4)
    ]
    for copy in loads + own_o:
        copy.start()
    for name in ("a1", "a0"):
        y_in[name].wait_recv()
        send_own(name.replace("a", "p"))

    def relay(step):
        zl, zr = lax.rem(z + NZ - step, NZ), lax.rem(z + step, NZ)
        for name in ("b0", "b1", "b2", "a1", "a0", "p1", "p0"):
            for source, zs, to, last in ((from_l, zl, to_r, ("b0", "a1", "a0")), (from_r, zr, to_l, ("b1", "b2", "p1", "p0"))):
                source[name, step].wait_recv()
                if step < 3 or name in last:
                    source[name, step + 1] = send(name, zs, to)
                if name[0] == "b":
                    y_in[name, step, to is to_r] = send(name, zs, to_y)
            if step == 1 and name == "b0":
                near.extend([a_send(1, to_xr), a_send(0, to_xl)])

    relay(1)
    near[0].wait_recv()
    far = [go.start(a_slot(xl, 0), a_slot(xl, 0), to_xr)]
    near[1].wait_recv()
    far.append(go.start(a_slot(xr, 1), a_slot(xr, 1), to_xl))
    halo_in.wait_recv()
    halo_own = abuf.at[x, pl.ds(0, HALO), lanes]
    halos = [go.start(halo_own, halo_own, to) for to in (to_xr, to_xl, to_xo)]
    mates = [go.start(a_slot(xl, 0), a_slot(xl, 0), mate), go.start(a_slot(xr, 1), a_slot(xr, 1), mate)]
    for copy in loads:
        copy.wait()
    f16buf[...] = f32buf[...].astype(BF).reshape(NX, 16, 16, BLK)
    relay(2)
    for copy in halos:
        copy.wait_recv()
    halo_all = abuf.at[:, pl.ds(0, HALO), lanes]
    mates.append(go.start(halo_all, halo_all, mate))
    relay(3)

    def to_owners(src, dst, sem):
        def one(t, carry):
            c = lax.rem(ctx + t, 64)
            yt, xt, zt = lax.div(c, 32), lax.rem(lax.div(c, 8), 4), lax.rem(c, 8)
            pltpu.make_async_remote_copy(
                src_ref=src(xt, yt * NZ + zt),
                dst_ref=dst,
                send_sem=all_send.at[sem],
                recv_sem=all_recv.at[sem],
                device_id={"ctx": c},
                device_id_type=MESH,
            ).start()
            return carry

        lax.fori_loop(1, 64, one, 0)
        own = pltpu.make_async_copy(src(x, me), dst, own_sem.at[sem])
        own.start()
        return own

    def from_owners(dst, sem):
        arrived = dst.at[pl.ds(0, 63)]
        pltpu.make_async_copy(arrived, arrived, all_recv.at[sem]).wait()

    own_f = to_owners(lambda xt, at: f16buf.at[xt, at], frecv.at[me * NX + x], 1)
    for copy, block, part in ((near[2], xl, 1), (near[3], xr, 0), (far[0], xo, 0), (far[1], xo, 1)):
        copy.wait_recv()
        mates.append(go.start(a_slot(block, part), a_slot(block, part), mate))
    zo = lax.rem(z + 4, NZ)
    for name in ("b0", "b1", "b2", "a1", "p1", "a0", "p0"):
        (from_l if name in ("b0", "a1", "a0") else from_r)[name, 4].wait_recv()
        if name[0] == "b":
            y_in[name, 4] = send(name, zo, to_y)
    for name, copy in y_in.items():
        if name not in ("a0", "a1"):
            copy.wait_recv()
    for copy in mates:
        copy.wait_recv()
    own_a.wait()

    def block(xb, carry):
        keep = jnp.where(yl * 32 + xb * 8 + z == 0, 0.0, 1.0).astype(F32)
        a = abuf[xb]
        filtered = []
        for j in range(3):
            wj = wbuf[j].reshape(D, CQ)
            bs[j] = jnp.dot(a, wj, preferred_element_type=F32).astype(BF).astype(F32)
            bs[j, pl.ds(0, HALO)] = bs[j, pl.ds(0, HALO)] * keep
            mine = pl.ds(pl.multiple_of(x * CQ, CQ), CQ)
            total = taps[j, pl.ds(0, 1), mine] * bs[j, pl.ds(HALO, BLK)]
            for k in range(1, TAPS):
                total = total + taps[j, pl.ds(k, 1), mine] * bs[j, pl.ds(HALO - k, BLK)]
            filtered.append(total)
        drv[:, xb] = (filtered[0] * filtered[2]).T.astype(BF).reshape(16, 16, BLK)
        spread(lambda p: drv.at[p, xb], drecv.at[me, xb], 0)
        qry[xb] = filtered[1].T.astype(BF)
        return carry

    lax.fori_loop(0, NX, block, 0)
    own_d = pltpu.make_async_copy(drv.at[me], drecv.at[me], own_sem.at[0])
    own_d.start()
    own_q = pltpu.make_async_copy(qry.at[x], qrecv.at[x], local_sem.at[0])
    own_q.start()
    q_in = [go.start(qry.at[xp], qrecv.at[x], to) for xp, to in ((xr, to_xr), (xl, to_xl), (xo, to_xo))]

    def inner(high, low, columns):
        return (
            jnp.dot(high, wide_h[:, columns], preferred_element_type=F32)
            + jnp.dot(low, wide_h[:, columns], preferred_element_type=F32)
            + jnp.dot(high, wide_l[:, columns], preferred_element_type=F32)
        )

    def widen(source):
        for side in range(2):
            half = source[:, :, 128 * side : 128 * side + 128]
            wide[side] = half.astype(F32).reshape(1024, 128)

    def spectrum(first):
        parts = []
        for i in range(GROUP):
            rows = jnp.concatenate(
                [wide[side, pl.ds(first + i, 64, stride=16), :] for side in range(2)], axis=1
            ).astype(BF)
            both = jnp.dot(ahead[...], jnp.concatenate([rows, rows], axis=0), preferred_element_type=F32)
            pieces = []
            for side in range(2):
                at = slice(128 * side, 128 * side + 128)
                re, im, tr, ti = both[:64, at], both[64:, at], turn[0, :, at], turn[1, :, at]
                pieces += [re * tr - im * ti, re * ti + im * tr]
            parts.append(jnp.concatenate(pieces, axis=1))
        return inner(*split(jnp.concatenate(parts, axis=0)), slice(None))

    def filter_group(g, carry):
        spec[g] = spectrum(g * GROUP)
        return carry

    def signal_group(g, carry):
        s = spectrum(g * GROUP)
        for side in range(2):
            re, im = slice(256 * side, 256 * side + 128), slice(256 * side + 128, 256 * side + 256)
            sr, si, hr, hi = s[:, re], s[:, im], spec[g, :, re], spec[g, :, im]
            p_high[g, :, re], p_low[g, :, re] = split(sr * hr - si * hi)
            p_high[g, :, im], p_low[g, :, im] = split(-(sr * hi + si * hr))
        return carry

    def inverse_group(side):
        at = slice(128 * side, 128 * side + 128)

        def one(g, carry):
            v = inner(p_high[g], p_low[g], slice(256 * side, 256 * side + 256))
            for i in range(0, GROUP, 2):
                pair = []
                for c in (i, i + 1):
                    re, im = v[64 * c : 64 * c + 64, :128], -v[64 * c : 64 * c + 64, 128:]
                    tr, ti = turn[0, :, at], turn[1, :, at]
                    pair.append(jnp.concatenate([re * tr + im * ti, im * tr - re * ti], axis=0))
                high, low = split(jnp.concatenate(pair, axis=1))
                y = jnp.dot(back[...], jnp.concatenate([high, low, high], axis=0), preferred_element_type=F32)
                out32[side, pl.ds(g * GROUP + i, 64, stride=16), :] = y[:, :128]
                out32[side, pl.ds(g * GROUP + i + 1, 64, stride=16), :] = y[:, 128:]
            return carry

        return one

    own_f.wait()
    from_owners(frecv, 1)
    widen(frecv[...])
    lax.fori_loop(0, 16 // GROUP, filter_group, 0)
    own_d.wait()
    pltpu.make_async_copy(drecv.at[pl.ds(0, 15)], drecv.at[pl.ds(0, 15)], all_recv.at[0]).wait()
    widen(drecv[...].reshape(64, 16, BLK))
    lax.fori_loop(0, 16 // GROUP, signal_group, 0)

    slot = x * 16 + me
    own_c = []
    for side in range(2):
        lax.fori_loop(0, 16 // GROUP, inverse_group(side), 0)
        osend[side] = out32[side].reshape(64, 16, 128).astype(BF)

        own_c.append(
            to_owners(lambda xt, at, side=side: osend.at[side, at * NX + xt], crecv.at[side, slot], 2 + side)
        )

    own_q.wait()
    for copy in q_in:
        copy.wait_recv()
    for copy in own_o:
        copy.wait()

    far_h, near_h = (1 - yh) * 2, yh * 2
    p_in, y_copy = {}, []
    for side in range(2):
        own_c[side].wait()
        from_owners(crecv.at[side], 2 + side)
        query = qrecv[:, :, 128 * side : 128 * side + 128].reshape(1024, 128).astype(F32)
        gated = (query * crecv[side].reshape(1024, 128).astype(F32)).T.astype(BF)

        def partial(h):
            return jnp.dot(gated, obuf[h], preferred_element_type=F32)

        psend[side, 0] = partial(far_h + 1 - core).astype(BF)
        p_in[side, 0] = go.start(psend.at[side, 0], precv.at[side, 0], mate)
        total = partial(far_h + core)
        p_in[side, 0].wait_recv()
        ysend[side] = (total + precv[side, 0].astype(F32)).astype(BF)
        y_copy.append(go.start(ysend.at[side], yrecv.at[side], across))
        psend[side, 1] = partial(near_h + 1 - core).astype(BF)
        p_in[side, 1] = go.start(psend.at[side, 1], precv.at[side, 1], mate)
        held[side] = partial(near_h + core)
    for side in range(2):
        p_in[side, 1].wait_recv()
        y_copy[side].wait_recv()
        total = held[side] + precv[side, 1].astype(F32) + yrecv[side].astype(F32)
        out[pl.ds(128 * side, 128), :] = total.astype(BF)

    go.wait_sends()
    pltpu.make_async_copy(drv.at[pl.ds(0, 15)], drv.at[pl.ds(0, 15)], all_send.at[0]).wait()
    pltpu.make_async_copy(frecv.at[pl.ds(0, 63)], frecv.at[pl.ds(0, 63)], all_send.at[1]).wait()
    for side in range(2):
        part = osend.at[side, pl.ds(0, 63)]
        pltpu.make_async_copy(part, part, all_send.at[2 + side]).wait()


def layer(act, w, taps, flt, w_out):
    any_space, vmem = pl.BlockSpec(memory_space=pl.ANY), pl.BlockSpec(memory_space=pltpu.VMEM)
    return pl.pallas_call(
        layer_kernel,
        out_shape=jax.ShapeDtypeStruct((BLK, 1024), BF),
        in_specs=[any_space] * 10,
        out_specs=vmem,
        scratch_shapes=[
            pltpu.VMEM((3, TAPS, 1024), F32),
            pltpu.VMEM((128, 128), BF),
            pltpu.VMEM((2, 64, BLK), F32),
            pltpu.VMEM((2 * BLK, 2 * BLK), BF),
            pltpu.VMEM((2 * BLK, 2 * BLK), BF),
            pltpu.VMEM((64, 384), BF),
            pltpu.VMEM((NX, ROWS, D), BF),
            pltpu.VMEM((3, NY, NX, NZ, DB, CQ), BF),
            pltpu.VMEM((3, ROWS, CQ), F32),
            pltpu.VMEM((1024, BLK), F32),
            pltpu.VMEM((NX, 16, 16, BLK), BF),
            pltpu.VMEM((64, 16, BLK), BF),
            pltpu.VMEM((16, NX, 16, BLK), BF),
            pltpu.VMEM((16, NX, 16, BLK), BF),
            pltpu.VMEM((NX, CQ, BLK), BF),
            pltpu.VMEM((NX, CQ, BLK), BF),
            pltpu.VMEM((2, 1024, 128), F32),
            pltpu.VMEM((2, 1024, 128), F32),
            pltpu.VMEM((16 // GROUP, 64 * GROUP, 2 * BLK), F32),
            pltpu.VMEM((16 // GROUP, 64 * GROUP, 2 * BLK), BF),
            pltpu.VMEM((16 // GROUP, 64 * GROUP, 2 * BLK), BF),
            pltpu.VMEM((2, 64, 16, 128), BF),
            pltpu.VMEM((2, 64, 16, 128), BF),
            pltpu.VMEM((4, 1024, 1024), BF),
            pltpu.VMEM((2, 2, 128, 1024), BF),
            pltpu.VMEM((2, 2, 128, 1024), BF),
            pltpu.VMEM((2, 128, 1024), BF),
            pltpu.VMEM((2, 128, 1024), BF),
            pltpu.VMEM((2, 128, 1024), F32),
            pltpu.SemaphoreType.DMA((16,)),
            pltpu.SemaphoreType.DMA((4,)),
            pltpu.SemaphoreType.DMA((4,)),
            pltpu.SemaphoreType.DMA((4,)),
            pltpu.SemaphoreType.DMA((N_COPIES,)),
            pltpu.SemaphoreType.DMA((N_COPIES,)),
        ],
        compiler_params=pltpu.CompilerParams(
            collective_id=0, has_side_effects=True, vmem_limit_bytes=58 * 1024 * 1024
        ),
        name="layer",
    )(act, w, taps, flt, w_out, *[jnp.asarray(table) for table in tables()])


def on_device(activations, w_in, short_taps, long_filter, w_out):
    return layer(activations, w_in, short_taps.transpose(0, 2, 1), long_filter, w_out)


def solution(mesh):
    return jax.shard_map(
        on_device,
        mesh=mesh,
        in_specs=(
            P("ctx", None),
            P(None, "ctx", "hid"),
            P(None, "hid", None),
            P("hid", "ctx"),
            P("hid", None),
        ),
        out_specs=P("ctx", "hid"),
        check_vma=False,
    )
```

```python
import math

import numpy as np
import ml_dtypes
import jax
import jax.numpy as jnp
from jax import lax
from jax.experimental import pallas as pl
from jax.experimental.pallas import tpu as pltpu
from jax.sharding import PartitionSpec as P

MESH = pl.DeviceIdType.MESH
BF = jnp.bfloat16
F32 = jnp.float32
TAPS = 3
NY, NX, NZ = 2, 4, 8
BLK = 256
HALO = 16
ROWS = BLK + HALO
D = 4096
CQ = 256
DB = 64


def place():
    ctx = lax.axis_index("ctx")
    hid = lax.axis_index("hid")
    yl = lax.div(ctx, 32)
    x = lax.rem(lax.div(ctx, 8), 4)
    z = lax.rem(ctx, 8)
    return ctx, hid, yl, x, z


def at_ctx(yl, x, z):
    return {"ctx": yl * 32 + x * 8 + z}


class Copies:
    def __init__(self, send, recv):
        self.send, self.recv, self.all = send, recv, []

    def start(self, src, dst, device):
        k = len(self.all)
        copy = pltpu.make_async_remote_copy(
            src_ref=src,
            dst_ref=dst,
            send_sem=self.send.at[k],
            recv_sem=self.recv.at[k],
            device_id=device,
            device_id_type=MESH,
        )
        copy.start()
        self.all.append(copy)
        return copy

    def wait_sends(self):
        for copy in self.all:
            copy.wait_send()


def halves(table):
    high = table.astype(ml_dtypes.bfloat16)
    low = (table - high.astype(np.float64)).astype(ml_dtypes.bfloat16)
    return high, low


def tables():
    order = np.array([yl * 32 + x * 8 + z for yl in range(NY) for z in range(NZ) for x in range(NX)])
    k1 = np.arange(64) + 0.5
    angle = 2 * np.pi * np.outer(k1, np.arange(64)) / 128
    ahead = np.concatenate([np.cos(angle), -np.sin(angle)], axis=0)
    back = np.concatenate([np.cos(angle.T), -np.sin(angle.T)], axis=1) * 2.0**-14
    turn = 2 * np.pi * np.outer(k1, np.arange(BLK)) / 32768
    inner = 2 * np.pi * (np.outer(np.arange(BLK), np.arange(BLK)) % BLK) / BLK
    c, s = np.cos(inner), np.sin(inner)
    wide = np.block([[c, -s], [s, c]])
    sides = np.array([part * BLK + side * 128 + i for side in range(2) for part in range(2) for i in range(128)])
    wide = wide[sides][:, sides]
    ahead_h, ahead_l = halves(ahead[:, order])
    back_h, back_l = halves(back[order])
    wide_h, wide_l = halves(wide)
    return (
        np.concatenate([ahead_h, ahead_l], axis=1),
        np.stack([np.cos(turn), -np.sin(turn)]).astype(np.float32),
        wide_h,
        wide_l,
        np.concatenate([back_h, back_h, back_l], axis=1),
    )


N_COPIES = 120
UNITS = {"b0": (0, 0, 3), "b1": (1, 0, 3), "b2": (3, 2, 1), "a0": (2, 0, 3), "a1": (3, 0, 2)}
GROUP = 4


def split(value):
    high = value.astype(BF)
    return high, (value - high.astype(F32)).astype(BF)


def layer_kernel(
    act, w, taps_in, flt, w_out, ahead_in, turn_in, wide_h_in, wide_l_in, back_in, out,
    taps, ahead, turn, wide_h, wide_l, back, abuf, wbuf, bs, f32buf, f16buf, frecv, drv, drecv, qry, qrecv, wide, out32, spec, p_high, p_low, osend, crecv,
    obuf, psend, precv, ysend, yrecv, held, local_sem, own_sem, all_send, all_recv, send_sem, recv_sem,
):
    tables_here = (
        (taps_in, taps), (ahead_in, ahead), (turn_in, turn), (wide_h_in, wide_h), (wide_l_in, wide_l), (back_in, back)
    )
    ctx, hid, yl, x, z = place()
    core = lax.rem(hid, 2)
    yh = lax.div(hid, 2)
    mate = {"hid": hid + 1 - 2 * core}
    across = {"hid": lax.rem(hid + 2, 4)}
    me = yl * NZ + z
    right, left = lax.rem(z + 1, NZ), lax.rem(z + NZ - 1, NZ)
    xr, xl, xo = lax.rem(x + 1, NX), lax.rem(x + 3, NX), lax.rem(x + 2, NX)
    after, before = lax.rem(ctx + 1, 64), lax.rem(ctx + 63, 64)
    to_r, to_l = at_ctx(yl, x, right), at_ctx(yl, x, left)
    to_y = at_ctx(1 - yl, x, z)
    to_xr, to_xl, to_xo = at_ctx(yl, xr, z), at_ctx(yl, xl, z), at_ctx(yl, xo, z)

    own_w = pltpu.make_async_copy(
        w.at[:, :, pl.ds(pl.multiple_of(x * CQ, CQ), CQ)], wbuf.at[:, yl, x, z], local_sem.at[0]
    )
    own_a = pltpu.make_async_copy(act, abuf.at[x, pl.ds(HALO, BLK)], local_sem.at[1])
    own_w.start()
    own_a.start()

    barrier = pltpu.get_barrier_semaphore()
    for peer in (to_xr, to_xl, to_xo, to_r, to_l, to_y, mate, across, {"ctx": after}, {"ctx": before}):
        pl.semaphore_signal(barrier, inc=1, device_id=peer, device_id_type=MESH)
    pl.semaphore_wait(barrier, 10)

    go = Copies(send_sem, recv_sem)

    def spread(src, dst, sem):
        def one(t, carry):
            p = lax.rem(me + t, 16)
            pltpu.make_async_remote_copy(
                src_ref=src(p),
                dst_ref=dst,
                send_sem=all_send.at[sem],
                recv_sem=all_recv.at[sem],
                device_id=at_ctx(lax.div(p, NZ), x, lax.rem(p, NZ)),
                device_id_type=MESH,
            ).start()
            return carry

        lax.fori_loop(1, 16, one, 0)

    first = []
    for xp, to in ((xr, to_xr), (xl, to_xl), (xo, to_xo)):
        first.append(
            go.start(w.at[:, :, pl.ds(pl.multiple_of(xp * CQ, CQ), CQ)], wbuf.at[:, yl, x, z], to)
        )

    def unit(name, zs):
        ys = 1 - yl if name[0] == "p" else yl
        xs, j, count = UNITS[name.replace("p", "a")]
        return wbuf.at[pl.ds(j, count), ys, lax.rem(x + xs, NX), zs]

    def send(name, zs, to):
        part = unit(name, zs)
        return go.start(part, part, to)

    from_l, from_r, y_in = {}, {}, {}

    def send_own(name):
        from_l[name, 1] = send(name, z, to_r)
        from_r[name, 1] = send(name, z, to_l)

    loads = [pltpu.make_async_copy(flt, f32buf, local_sem.at[2])]
    for k, (table, kept) in enumerate(tables_here):
        loads.append(pltpu.make_async_copy(table, kept, local_sem.at[7 + k]))
    own_o = [
        pltpu.make_async_copy(w_out.at[:, pl.ds(1024 * h, 1024)], obuf.at[h], local_sem.at[3 + h])
        for h in range(4)
    ]
    for copy in loads:
        copy.start()
    own_w.wait()
    send_own("b0")
    y_in["b0"] = send("b0", z, to_y)
    x_next = lax.rem(lax.div(after, 8), 4)
    lanes = pl.ds(pl.multiple_of(core * (D // 2), D // 2), D // 2)
    halo_in = go.start(
        act.at[pl.ds(BLK - HALO, HALO), lanes], abuf.at[x_next, pl.ds(0, HALO), lanes], {"ctx": after}
    )
    first[1].wait_recv()
    send_own("b1")
    y_in["b1"] = send("b1", z, to_y)
    first[0].wait_recv()
    y_in["a1"] = send("a1", z, to_y)
    send_own("b2")
    y_in["b2"] = send("b2", z, to_y)
    first[2].wait_recv()
    y_in["a0"] = send("a0", z, to_y)
    send_own("a1")
    send_own("a0")

    def a_rows(part):
        return pl.multiple_of(core * 128 + part * 64, 64)

    def a_slot(block, part, count=64):
        return abuf.at[block, pl.ds(pl.multiple_of(HALO + core * 128 + part * 64, 16), count)]

    def a_send(part, to):
        return go.start(act.at[pl.ds(a_rows(part), 64)], a_slot(x, part), to)

    near = [a_send(0, to_xr), a_send(1, to_xl)]
    for copy in loads:
        copy.wait()
    f16buf[...] = f32buf[...].astype(BF).reshape(NX, 16, 16, BLK)
    for name in ("a1", "a0"):
        y_in[name].wait_recv()
        send_own(name.replace("a", "p"))
    far, halos, mates = [], [], []

    def far_half():
        near[0].wait_recv()
        far.append(go.start(a_slot(xl, 0), a_slot(xl, 0), to_xr))
        near[1].wait_recv()
        far.append(go.start(a_slot(xr, 1), a_slot(xr, 1), to_xl))
        halo_in.wait_recv()
        halo_own = abuf.at[x, pl.ds(0, HALO), lanes]
        halos.extend([go.start(halo_own, halo_own, to) for to in (to_xr, to_xl, to_xo)])
        for block, part in ((xl, 0), (xr, 1)):
            mates.append(go.start(a_slot(block, part), a_slot(block, part), mate))

    def relay(step):
        zl, zr = lax.rem(z + NZ - step, NZ), lax.rem(z + step, NZ)
        for name in ("b0", "b1", "b2", "a1", "a0", "p1", "p0"):
            for source, zs, to, last in ((from_l, zl, to_r, ("b0", "a1", "a0")), (from_r, zr, to_l, ("b1", "b2", "p1", "p0"))):
                source[name, step].wait_recv()
                if step < 3 or name in last:
                    source[name, step + 1] = send(name, zs, to)
                if name[0] == "b":
                    y_in[name, step, to is to_r] = send(name, zs, to_y)
            if step == 1 and name == "b0":
                near.extend([a_send(1, to_xr), a_send(0, to_xl)])
            if step == 2 and name == "a0":
                far_half()

    relay(1)
    for copy in own_o:
        copy.start()
    relay(2)
    relay(3)
    for copy in halos:
        copy.wait_recv()
    halo_all = abuf.at[:, pl.ds(0, HALO), lanes]
    halo_mate = go.start(halo_all, halo_all, mate)

    def to_owners(src, dst, sem):
        def one(t, carry):
            c = lax.rem(ctx + t, 64)
            yt, xt, zt = lax.div(c, 32), lax.rem(lax.div(c, 8), 4), lax.rem(c, 8)
            pltpu.make_async_remote_copy(
                src_ref=src(xt, yt * NZ + zt),
                dst_ref=dst,
                send_sem=all_send.at[sem],
                recv_sem=all_recv.at[sem],
                device_id={"ctx": c},
                device_id_type=MESH,
            ).start()
            return carry

        lax.fori_loop(1, 64, one, 0)
        own = pltpu.make_async_copy(src(x, me), dst, own_sem.at[sem])
        own.start()
        return own

    def from_owners(dst, sem):
        arrived = dst.at[pl.ds(0, 63)]
        pltpu.make_async_copy(arrived, arrived, all_recv.at[sem]).wait()

    zo = lax.rem(z + 4, NZ)
    last = {"b0": from_l, "b1": from_r, "b2": from_r, "a1": from_l, "a0": from_l, "p1": from_r, "p0": from_r}
    for name in ("b0", "b1", "b2"):
        last[name][name, 4].wait_recv()
        y_in[name, 4] = send(name, zo, to_y)
    own_f = to_owners(lambda xt, at: f16buf.at[xt, at], frecv.at[me * NX + x], 1)
    for copy, block, part in ((near[2], xl, 1), (near[3], xr, 0), (far[0], xo, 0), (far[1], xo, 1)):
        copy.wait_recv()
        mates.append(go.start(a_slot(block, part), a_slot(block, part), mate))
    for name in ("a1", "a0", "p1", "p0"):
        last[name][name, 4].wait_recv()
    for name, copy in y_in.items():
        if name not in ("a0", "a1"):
            copy.wait_recv()
    halo_mate.wait_recv()
    own_a.wait()

    def block(xb, carry):
        keep = jnp.where(yl * 32 + xb * 8 + z == 0, 0.0, 1.0).astype(F32)
        a = abuf[xb]
        filtered = []
        for j in range(3):
            wj = wbuf[j].reshape(D, CQ)
            bs[j] = jnp.dot(a, wj, preferred_element_type=F32).astype(BF).astype(F32)
            bs[j, pl.ds(0, HALO)] = bs[j, pl.ds(0, HALO)] * keep
            mine = pl.ds(pl.multiple_of(x * CQ, CQ), CQ)
            total = taps[j, pl.ds(0, 1), mine] * bs[j, pl.ds(HALO, BLK)]
            for k in range(1, TAPS):
                total = total + taps[j, pl.ds(k, 1), mine] * bs[j, pl.ds(HALO - k, BLK)]
            filtered.append(total)
        drv[:, xb] = (filtered[0] * filtered[2]).T.astype(BF).reshape(16, 16, BLK)
        spread(lambda p: drv.at[p, xb], drecv.at[me, xb], 0)
        qry[xb] = filtered[1].T.astype(BF)
        return carry

    block(x, 0)
    for copy in mates:
        copy.wait_recv()
    lax.fori_loop(1, NX, lambda t, carry: block(lax.rem(x + t, NX), carry), 0)
    own_d = pltpu.make_async_copy(drv.at[me], drecv.at[me], own_sem.at[0])
    own_d.start()
    own_q = pltpu.make_async_copy(qry.at[x], qrecv.at[x], local_sem.at[0])
    own_q.start()
    q_in = [go.start(qry.at[xp], qrecv.at[x], to) for xp, to in ((xr, to_xr), (xl, to_xl), (xo, to_xo))]

    def inner(high, low, columns):
        return (
            jnp.dot(high, wide_h[:, columns], preferred_element_type=F32)
            + jnp.dot(low, wide_h[:, columns], preferred_element_type=F32)
            + jnp.dot(high, wide_l[:, columns], preferred_element_type=F32)
        )

    def widen(source):
        for side in range(2):
            half = source[:, :, 128 * side : 128 * side + 128]
            wide[side] = half.astype(F32).reshape(1024, 128)

    def spectrum(first):
        parts = []
        for i in range(GROUP):
            rows = jnp.concatenate(
                [wide[side, pl.ds(first + i, 64, stride=16), :] for side in range(2)], axis=1
            ).astype(BF)
            both = jnp.dot(ahead[...], jnp.concatenate([rows, rows], axis=0), preferred_element_type=F32)
            pieces = []
            for side in range(2):
                at = slice(128 * side, 128 * side + 128)
                re, im, tr, ti = both[:64, at], both[64:, at], turn[0, :, at], turn[1, :, at]
                pieces += [re * tr - im * ti, re * ti + im * tr]
            parts.append(jnp.concatenate(pieces, axis=1))
        return inner(*split(jnp.concatenate(parts, axis=0)), slice(None))

    def filter_group(g, carry):
        spec[g] = spectrum(g * GROUP)
        return carry

    def signal_group(g, carry):
        s = spectrum(g * GROUP)
        for side in range(2):
            re, im = slice(256 * side, 256 * side + 128), slice(256 * side + 128, 256 * side + 256)
            sr, si, hr, hi = s[:, re], s[:, im], spec[g, :, re], spec[g, :, im]
            p_high[g, :, re], p_low[g, :, re] = split(sr * hr - si * hi)
            p_high[g, :, im], p_low[g, :, im] = split(-(sr * hi + si * hr))
        return carry

    def inverse_group(side):
        at = slice(128 * side, 128 * side + 128)

        def one(g, carry):
            v = inner(p_high[g], p_low[g], slice(256 * side, 256 * side + 256))
            for i in range(0, GROUP, 2):
                pair = []
                for c in (i, i + 1):
                    re, im = v[64 * c : 64 * c + 64, :128], -v[64 * c : 64 * c + 64, 128:]
                    tr, ti = turn[0, :, at], turn[1, :, at]
                    pair.append(jnp.concatenate([re * tr + im * ti, im * tr - re * ti], axis=0))
                high, low = split(jnp.concatenate(pair, axis=1))
                y = jnp.dot(back[...], jnp.concatenate([high, low, high], axis=0), preferred_element_type=F32)
                out32[side, pl.ds(g * GROUP + i, 64, stride=16), :] = y[:, :128]
                out32[side, pl.ds(g * GROUP + i + 1, 64, stride=16), :] = y[:, 128:]
            return carry

        return one

    own_f.wait()
    from_owners(frecv, 1)
    widen(frecv[...])
    lax.fori_loop(0, 16 // GROUP, filter_group, 0)
    own_d.wait()
    pltpu.make_async_copy(drecv.at[pl.ds(0, 15)], drecv.at[pl.ds(0, 15)], all_recv.at[0]).wait()
    widen(drecv[...].reshape(64, 16, BLK))
    lax.fori_loop(0, 16 // GROUP, signal_group, 0)

    slot = x * 16 + me
    own_c = []
    for side in range(2):
        lax.fori_loop(0, 16 // GROUP, inverse_group(side), 0)
        osend[side] = out32[side].reshape(64, 16, 128).astype(BF)

        own_c.append(
            to_owners(lambda xt, at, side=side: osend.at[side, at * NX + xt], crecv.at[side, slot], 2 + side)
        )

    own_q.wait()
    for copy in q_in:
        copy.wait_recv()
    for copy in own_o:
        copy.wait()

    far_h, near_h = (1 - yh) * 2, yh * 2
    p_in, y_copy = {}, []
    for side in range(2):
        own_c[side].wait()
        from_owners(crecv.at[side], 2 + side)
        query = qrecv[:, :, 128 * side : 128 * side + 128].reshape(1024, 128).astype(F32)
        gated = (query * crecv[side].reshape(1024, 128).astype(F32)).T.astype(BF)

        def partial(h):
            return jnp.dot(gated, obuf[h], preferred_element_type=F32)

        psend[side, 0] = partial(far_h + 1 - core).astype(BF)
        p_in[side, 0] = go.start(psend.at[side, 0], precv.at[side, 0], mate)
        total = partial(far_h + core)
        p_in[side, 0].wait_recv()
        ysend[side] = (total + precv[side, 0].astype(F32)).astype(BF)
        y_copy.append(go.start(ysend.at[side], yrecv.at[side], across))
        psend[side, 1] = partial(near_h + 1 - core).astype(BF)
        p_in[side, 1] = go.start(psend.at[side, 1], precv.at[side, 1], mate)
        held[side] = partial(near_h + core)
    for side in range(2):
        p_in[side, 1].wait_recv()
        y_copy[side].wait_recv()
        total = held[side] + precv[side, 1].astype(F32) + yrecv[side].astype(F32)
        out[pl.ds(128 * side, 128), :] = total.astype(BF)

    go.wait_sends()
    pltpu.make_async_copy(drv.at[pl.ds(0, 15)], drv.at[pl.ds(0, 15)], all_send.at[0]).wait()
    pltpu.make_async_copy(frecv.at[pl.ds(0, 63)], frecv.at[pl.ds(0, 63)], all_send.at[1]).wait()
    for side in range(2):
        part = osend.at[side, pl.ds(0, 63)]
        pltpu.make_async_copy(part, part, all_send.at[2 + side]).wait()


def layer(act, w, taps, flt, w_out):
    any_space, vmem = pl.BlockSpec(memory_space=pl.ANY), pl.BlockSpec(memory_space=pltpu.VMEM)
    return pl.pallas_call(
        layer_kernel,
        out_shape=jax.ShapeDtypeStruct((BLK, 1024), BF),
        in_specs=[any_space] * 10,
        out_specs=vmem,
        scratch_shapes=[
            pltpu.VMEM((3, TAPS, 1024), F32),
            pltpu.VMEM((128, 128), BF),
            pltpu.VMEM((2, 64, BLK), F32),
            pltpu.VMEM((2 * BLK, 2 * BLK), BF),
            pltpu.VMEM((2 * BLK, 2 * BLK), BF),
            pltpu.VMEM((64, 384), BF),
            pltpu.VMEM((NX, ROWS, D), BF),
            pltpu.VMEM((3, NY, NX, NZ, DB, CQ), BF),
            pltpu.VMEM((3, ROWS, CQ), F32),
            pltpu.VMEM((1024, BLK), F32),
            pltpu.VMEM((NX, 16, 16, BLK), BF),
            pltpu.VMEM((64, 16, BLK), BF),
            pltpu.VMEM((16, NX, 16, BLK), BF),
            pltpu.VMEM((16, NX, 16, BLK), BF),
            pltpu.VMEM((NX, CQ, BLK), BF),
            pltpu.VMEM((NX, CQ, BLK), BF),
            pltpu.VMEM((2, 1024, 128), F32),
            pltpu.VMEM((2, 1024, 128), F32),
            pltpu.VMEM((16 // GROUP, 64 * GROUP, 2 * BLK), F32),
            pltpu.VMEM((16 // GROUP, 64 * GROUP, 2 * BLK), BF),
            pltpu.VMEM((16 // GROUP, 64 * GROUP, 2 * BLK), BF),
            pltpu.VMEM((2, 64, 16, 128), BF),
            pltpu.VMEM((2, 64, 16, 128), BF),
            pltpu.VMEM((4, 1024, 1024), BF),
            pltpu.VMEM((2, 2, 128, 1024), BF),
            pltpu.VMEM((2, 2, 128, 1024), BF),
            pltpu.VMEM((2, 128, 1024), BF),
            pltpu.VMEM((2, 128, 1024), BF),
            pltpu.VMEM((2, 128, 1024), F32),
            pltpu.SemaphoreType.DMA((16,)),
            pltpu.SemaphoreType.DMA((4,)),
            pltpu.SemaphoreType.DMA((4,)),
            pltpu.SemaphoreType.DMA((4,)),
            pltpu.SemaphoreType.DMA((N_COPIES,)),
            pltpu.SemaphoreType.DMA((N_COPIES,)),
        ],
        compiler_params=pltpu.CompilerParams(
            collective_id=0, has_side_effects=True, vmem_limit_bytes=58 * 1024 * 1024
        ),
        name="layer",
    )(act, w, taps, flt, w_out, *[jnp.asarray(table) for table in tables()])


def on_device(activations, w_in, short_taps, long_filter, w_out):
    return layer(activations, w_in, short_taps.transpose(0, 2, 1), long_filter, w_out)


def solution(mesh):
    return jax.shard_map(
        on_device,
        mesh=mesh,
        in_specs=(
            P("ctx", None),
            P(None, "ctx", "hid"),
            P(None, "hid", None),
            P("hid", "ctx"),
            P("hid", None),
        ),
        out_specs=P("ctx", "hid"),
        check_vma=False,
    )
```

```python
import math

import numpy as np
import ml_dtypes
import jax
import jax.numpy as jnp
from jax import lax
from jax.experimental import pallas as pl
from jax.experimental.pallas import tpu as pltpu
from jax.sharding import PartitionSpec as P

MESH = pl.DeviceIdType.MESH
BF = jnp.bfloat16
F32 = jnp.float32
TAPS = 3
NY, NX, NZ = 2, 4, 8
BLK = 256
D = 4096
CG = 128
DB = 64


HOOK = 3


def place():
    ctx = lax.axis_index("ctx")
    hid = lax.axis_index("hid")
    yl = lax.div(ctx, 32)
    x = lax.rem(lax.div(ctx, 8), 4)
    z = lax.rem(ctx, 8)
    return ctx, hid, yl, x, z


def at_ctx(yl, x, z):
    return {"ctx": yl * 32 + x * 8 + z}


class Copies:
    def __init__(self, send, recv):
        self.send, self.recv, self.all = send, recv, []

    def start(self, src, dst, device):
        k = len(self.all)
        copy = pltpu.make_async_remote_copy(
            src_ref=src,
            dst_ref=dst,
            send_sem=self.send.at[k],
            recv_sem=self.recv.at[k],
            device_id=device,
            device_id_type=MESH,
        )
        copy.start()
        self.all.append(copy)
        return copy

    def wait_sends(self):
        for copy in self.all:
            copy.wait_send()


def halves(table):
    high = table.astype(ml_dtypes.bfloat16)
    low = (table - high.astype(np.float64)).astype(ml_dtypes.bfloat16)
    return high, low


def tables():
    order = np.array([yl * 32 + x * 8 + z for z in range(NZ) for yl in range(NY) for x in range(NX)])
    k1 = np.arange(64) + 0.5
    angle = 2 * np.pi * np.outer(k1, np.arange(64)) / 128
    ahead = np.concatenate([np.cos(angle), -np.sin(angle)], axis=0)
    back = np.concatenate([np.cos(angle.T), -np.sin(angle.T)], axis=1) * 2.0**-14
    turn = 2 * np.pi * np.outer(k1, np.arange(BLK)) / 32768
    inner = 2 * np.pi * (np.outer(np.arange(BLK), np.arange(BLK)) % BLK) / BLK
    c, s = np.cos(inner), np.sin(inner)
    wide = np.block([[c, -s], [s, c]])
    sides = np.array([part * BLK + side * 128 + i for side in range(2) for part in range(2) for i in range(128)])
    wide = wide[sides][:, sides]
    ahead_h, ahead_l = halves(ahead[:, order])
    back_h, back_l = halves(back[order])
    wide_h, wide_l = halves(wide)
    return (
        np.concatenate([ahead_h, ahead_l], axis=1),
        np.stack([np.cos(turn), -np.sin(turn)]).astype(np.float32),
        wide_h,
        wide_l,
        np.concatenate([back_h, back_l], axis=1),
    )


N_COPIES = 160
PLANE = [(0, 0), (1, 0), (0, 1), (0, 3), (0, 2), (1, 1), (1, 3), (1, 2)]
GROUP = 4


def split(value):
    high = value.astype(BF)
    return high, (value - high.astype(F32)).astype(BF)


def layer_kernel(
    act, w, taps_in, flt, w_out, ahead_in, turn_in, wide_h_in, wide_l_in, back_in, out,
    taps, ahead, turn, wide_h, wide_l, back, abuf, wbuf, last16, packed, halo_out, halo_in, halo_act, halo_br, bs, f32buf, f16buf, frecv, drv, drecv, qry, qrecv, wide, out32, spec, prod, osend, crecv,
    obuf, psend, precv, ysend, yrecv, held, local_sem, own_sem, all_send, all_recv, send_sem, recv_sem,
):
    tables_here = (
        (taps_in, taps), (ahead_in, ahead), (turn_in, turn), (wide_h_in, wide_h), (wide_l_in, wide_l), (back_in, back)
    )
    ctx, hid, yl, x, z = place()
    core = lax.rem(hid, 2)
    yh = lax.div(hid, 2)
    mate = {"hid": hid + 1 - 2 * core}
    across = {"hid": lax.rem(hid + 2, 4)}
    xr, xl, xo = lax.rem(x + 1, NX), lax.rem(x + 3, NX), lax.rem(x + 2, NX)
    after, before = lax.rem(z + 1, NZ), lax.rem(z + NZ - 1, NZ)
    to_r, to_l = at_ctx(yl, x, after), at_ctx(yl, x, before)
    to_xr, to_xl = at_ctx(yl, xr, z), at_ctx(yl, xl, z)
    to_s = at_ctx(1 - yl, x, z)
    to_o = {"ctx": (1 - yl) * 32 + x * 8 + z, "hid": lax.rem(hid + 2, 4)}
    mine = x * NY + yl

    def rel(dy, dx):
        return lax.rem(yl + dy, NY), lax.rem(x + dx, NX)

    def columns(y, xs):
        return pl.ds(pl.multiple_of((xs * NY + y) * CG, CG), CG)

    own_w = [
        pltpu.make_async_copy(
            w.at[j, :, columns(yl, x)], wbuf.at[yl, x, z, :, pl.ds(j * CG, CG)], local_sem.at[13 + j]
        )
        for j in range(3)
    ]
    own_a = pltpu.make_async_copy(act, abuf.at[yl, x], local_sem.at[1])
    tail = pltpu.make_async_copy(act.at[pl.ds(BLK - 16, 16)], last16, local_sem.at[0])
    for copy in own_w + [tail, own_a]:
        copy.start()

    barrier = pltpu.get_barrier_semaphore()
    peers = [mate, across, to_o] + [at_ctx(*rel(dy, dx), z) for dy, dx in PLANE[1:]]
    for dy, dx in PLANE:
        peers += [at_ctx(*rel(dy, dx), after), at_ctx(*rel(dy, dx), before)]
    for peer in peers:
        pl.semaphore_signal(barrier, inc=1, device_id=peer, device_id_type=MESH)
    pl.semaphore_wait(barrier, len(peers))

    go = Copies(send_sem, recv_sem)
    first = {}
    for dy, dx in PLANE[1:]:
        yt, xt = rel(dy, dx)
        first[dy, (NX - dx) % NX] = [
            go.start(
                w.at[j, :, columns(yt, xt)], wbuf.at[yl, x, z, :, pl.ds(j * CG, CG)], at_ctx(yt, xt, z)
            )
            for j in range(3)
        ]

    def send(unit, zs, to):
        yu, xu = rel(*unit)
        part = wbuf.at[yu, xu, zs]
        return go.start(part, part, to)

    from_l, from_r = {}, {}

    def send_own(unit):
        from_l[unit, 1] = send(unit, z, to_r)
        from_r[unit, 1] = send(unit, z, to_l)

    loads = [pltpu.make_async_copy(flt, f32buf, local_sem.at[2])]
    for k, (table, kept) in enumerate(tables_here):
        loads.append(pltpu.make_async_copy(table, kept, local_sem.at[7 + k]))
    own_o = [
        pltpu.make_async_copy(w_out.at[:, pl.ds(1024 * h, 1024)], obuf.at[h], local_sem.at[3 + h])
        for h in range(4)
    ]
    for copy in loads:
        copy.start()
    for copy in own_w:
        copy.wait()
    send_own((0, 0))

    tail.wait()
    rows = last16[...].astype(F32)
    for k in range(8):
        packed[pl.ds(2 * k, 2), :] = rows[14:16, 512 * k : 512 * k + 512]
    halo_out[...] = packed[...].astype(BF)
    halos = []
    x_next = lax.rem(x + lax.div(z + 1, NZ), NX)
    y_next = lax.rem(yl + lax.div(x * NZ + z + 1, NX * NZ), NY)
    for dy, dx in PLANE:
        halos.append(go.start(halo_out, halo_in.at[y_next, x_next], at_ctx(*rel(dy, dx), after)))

    for unit in PLANE[1:]:
        for copy in first[unit]:
            copy.wait_recv()
        send_own(unit)

    def a_slot(y, block, part, first_row=0, count=64):
        return abuf.at[y, block, pl.ds(pl.multiple_of(core * 128 + part * 64 + first_row, 16), count)]

    def a_send(part, to):
        return go.start(
            act.at[pl.ds(pl.multiple_of(core * 128 + part * 64, 64), 64)], a_slot(yl, x, part), to
        )

    y_in, mates = {}, {}

    def y_send(block, dx, part, count=32):
        for half, to in ((0, to_s), (1, to_o)):
            piece = a_slot(yl, block, part, half * count, count)
            y_in[dx, part, half] = go.start(piece, piece, to)

    def mate_own(block, dx, part):
        mates[0, dx, part] = go.start(a_slot(yl, block, part), a_slot(yl, block, part), mate)

    def mate_other(block, dx, part):
        y_in[dx, part, 0].wait_recv()
        y_in[dx, part, 1].wait_recv()
        if dx == 2:
            far_other[part].wait_recv()
        mates[1, dx, part] = go.start(a_slot(1 - yl, block, part), a_slot(1 - yl, block, part), mate)

    near = [a_send(0, to_xr), a_send(1, to_xl)]
    own_a.wait()
    y_send(x, 0, 0)
    y_send(x, 0, 1)
    for copy in loads:
        copy.wait()
    f16buf[...] = f32buf[...].astype(BF).reshape(8, NZ, 16, BLK)

    def relay(step):
        zl, zr = lax.rem(z + NZ - step, NZ), lax.rem(z + step, NZ)
        for k, unit in enumerate(PLANE):
            from_l[unit, step].wait_recv()
            if step < 3 or k % 2 == 0:
                from_l[unit, step + 1] = send(unit, zl, to_r)
            from_r[unit, step].wait_recv()
            if step < 3 or k % 2 == 1:
                from_r[unit, step + 1] = send(unit, zr, to_l)
            if k == HOOK and step in hooks:
                hooks[step]()

    def first_halves():
        near[0].wait_recv()
        y_send(xl, 3, 0)
        mate_own(xl, 3, 0)
        near[1].wait_recv()
        y_send(xr, 1, 1)
        mate_own(xr, 1, 1)
        far.append(go.start(a_slot(yl, xl, 0), a_slot(yl, xl, 0), to_xr))
        far.append(go.start(a_slot(yl, xr, 1), a_slot(yl, xr, 1), to_xl))

    def second_halves():
        near[2].wait_recv()
        y_send(xl, 3, 1)
        mate_own(xl, 3, 1)
        near[3].wait_recv()
        y_send(xr, 1, 0)
        mate_own(xr, 1, 0)

    far, far_other, hooks = [], [], {2: first_halves, 3: second_halves}
    relay(1)
    near += [a_send(1, to_xr), a_send(0, to_xl)]
    for copy in own_o:
        copy.start()
    relay(2)
    mate_other(x, 0, 0)
    mate_other(x, 0, 1)
    for copy in halos:
        copy.wait_recv()
    for y in range(NY):
        for xs in range(NX):
            got = halo_in[y, xs].astype(F32)
            for k in range(8):
                halo_act[pl.ds(2 * (y * NX + xs), 2), pl.ds(512 * k, 512)] = got[2 * k : 2 * k + 2]
    relay(3)
    mate_other(xl, 3, 0)
    mate_other(xr, 1, 1)
    for block, part, to in ((xl, 0, to_xr), (xr, 1, to_xl)):
        piece = a_slot(1 - yl, block, part, 32, 32)
        far_other.append(go.start(piece, piece, to))

    def to_owners(src, dst, sem):
        def one(t, carry):
            c = lax.rem(ctx + t, 64)
            yt, xt, zt = lax.div(c, 32), lax.rem(lax.div(c, 8), 4), lax.rem(c, 8)
            pltpu.make_async_remote_copy(
                src_ref=src(yt, xt, zt),
                dst_ref=dst,
                send_sem=all_send.at[sem],
                recv_sem=all_recv.at[sem],
                device_id={"ctx": c},
                device_id_type=MESH,
            ).start()
            return carry

        lax.fori_loop(1, 64, one, 0)
        own = pltpu.make_async_copy(src(yl, x, z), dst, own_sem.at[sem])
        own.start()
        return own

    def from_owners(dst, sem):
        arrived = dst.at[pl.ds(0, 63)]
        pltpu.make_async_copy(arrived, arrived, all_recv.at[sem]).wait()

    here = z * 8 + yl * NX + x
    own_f = to_owners(lambda yt, xt, zt: f16buf.at[xt * NY + yt, zt], frecv.at[here], 1)
    for k, unit in enumerate(PLANE):
        (from_l if k % 2 == 0 else from_r)[unit, 4].wait_recv()
    def await_mates(keys):
        for key in keys:
            for part in range(2):
                mates[(*key, part)].wait_recv()

    rims = jnp.dot(
        halo_act[...].astype(BF), wbuf[...].reshape(D, 3 * CG), preferred_element_type=F32
    ).astype(BF).astype(F32)
    halo_br[...] = jnp.zeros_like(halo_br)
    for b in range(8):
        halo_br[b, pl.ds(6, 2)] = rims[2 * b : 2 * b + 2]

    def block(yb, xb):
        at = yb * NX + xb
        keep = jnp.where(yb * 32 + xb * 8 + z == 0, 0.0, 1.0).astype(F32)
        bs[pl.ds(8, BLK)] = (
            jnp.dot(abuf[yb, xb], wbuf[...].reshape(D, 3 * CG), preferred_element_type=F32).astype(BF).astype(F32)
        )
        bs[pl.ds(0, 8)] = halo_br[at] * keep
        filtered = []
        for j in range(3):
            lanes = slice(j * CG, j * CG + CG)
            total = taps[j, pl.ds(0, 1), columns(yl, x)] * bs[pl.ds(8, BLK), lanes]
            for k in range(1, TAPS):
                total = total + taps[j, pl.ds(k, 1), columns(yl, x)] * bs[pl.ds(8 - k, BLK), lanes]
            filtered.append(total)
        drv[:, at] = (filtered[0] * filtered[2]).T.astype(BF).reshape(NZ, 16, BLK)

        def one(t, carry):
            zt = lax.rem(z + t, NZ)
            pltpu.make_async_remote_copy(
                src_ref=drv.at[zt, at],
                dst_ref=drecv.at[z, at],
                send_sem=all_send.at[0],
                recv_sem=all_recv.at[0],
                device_id=at_ctx(yl, x, zt),
                device_id_type=MESH,
            ).start()
            return carry

        lax.fori_loop(1, NZ, one, 0)
        qry[at] = filtered[1].T.astype(BF)

    def early(t, carry):
        block(lax.rem(yl + lax.div(t, 3), NY), lax.rem(x + t + lax.div(t, 2), NX))
        return carry

    def middle(t, carry):
        block(1 - yl, lax.rem(x + 1 + 2 * t, NX))
        return carry

    await_mates([(0, 1), (0, 3), (1, 0)])
    lax.fori_loop(0, 2, early, 0)
    for part in range(2):
        far[part].wait_recv()
        y_send(xo, 2, part, 16)
        mate_own(xo, 2, part)
    lax.fori_loop(2, 4, early, 0)


    mate_other(xl, 3, 1)
    mate_other(xr, 1, 0)
    await_mates([(1, 1), (1, 3), (0, 2)])
    lax.fori_loop(0, 2, middle, 0)
    block(yl, xo)
    mate_other(xo, 2, 0)
    mate_other(xo, 2, 1)
    await_mates([(1, 2)])
    block(1 - yl, xo)

    own_d = pltpu.make_async_copy(drv.at[z], drecv.at[z], own_sem.at[0])
    own_d.start()
    own_q = pltpu.make_async_copy(qry.at[yl * NX + x], qrecv.at[mine], local_sem.at[0])
    own_q.start()
    q_in = []
    for dy, dx in PLANE[1:]:
        yt, xt = rel(dy, dx)
        q_in.append(go.start(qry.at[yt * NX + xt], qrecv.at[mine], at_ctx(yt, xt, z)))

    def inner(high, columns):
        return jnp.dot(high, wide_h[:, columns], preferred_element_type=F32)

    def widen(source):
        for side in range(2):
            half = source[:, :, 128 * side : 128 * side + 128]
            wide[side] = half.astype(F32).reshape(1024, 128)

    def turned(first):
        parts = []
        for i in range(GROUP):
            rows = jnp.concatenate(
                [wide[side, pl.ds(first + i, 64, stride=16), :] for side in range(2)], axis=1
            ).astype(BF)
            both = jnp.dot(ahead[...], jnp.concatenate([rows, rows], axis=0), preferred_element_type=F32)
            pieces = []
            for side in range(2):
                at = slice(128 * side, 128 * side + 128)
                re, im, tr, ti = both[:64, at], both[64:, at], turn[0, :, at], turn[1, :, at]
                pieces += [re * tr - im * ti, re * ti + im * tr]
            parts.append(jnp.concatenate(pieces, axis=1))
        return jnp.concatenate(parts, axis=0)

    def filter_group(g, carry):
        high, low = split(turned(g * GROUP))
        spec[g] = (
            inner(high, slice(None))
            + inner(low, slice(None))
            + jnp.dot(high, wide_l[...], preferred_element_type=F32)
        )
        return carry

    def signal_group(g, carry):
        s = inner(turned(g * GROUP).astype(BF), slice(None))
        for side in range(2):
            re, im = slice(256 * side, 256 * side + 128), slice(256 * side + 128, 256 * side + 256)
            sr, si, hr, hi = s[:, re], s[:, im], spec[g, :, re], spec[g, :, im]
            prod[g, :, re] = (sr * hr - si * hi).astype(BF)
            prod[g, :, im] = -(sr * hi + si * hr).astype(BF)
        return carry

    def inverse_group(side):
        at = slice(128 * side, 128 * side + 128)

        def one(g, carry):
            v = inner(prod[g], slice(256 * side, 256 * side + 256))
            for i in range(0, GROUP, 2):
                pair = []
                for c in (i, i + 1):
                    re, im = v[64 * c : 64 * c + 64, :128], -v[64 * c : 64 * c + 64, 128:]
                    tr, ti = turn[0, :, at], turn[1, :, at]
                    pair.append(jnp.concatenate([re * tr + im * ti, im * tr - re * ti], axis=0))
                high = jnp.concatenate(pair, axis=1).astype(BF)
                y = jnp.dot(back[...], jnp.concatenate([high, high], axis=0), preferred_element_type=F32)
                out32[side, pl.ds(g * GROUP + i, 64, stride=16), :] = y[:, :128]
                out32[side, pl.ds(g * GROUP + i + 1, 64, stride=16), :] = y[:, 128:]
            return carry

        return one

    own_f.wait()
    from_owners(frecv, 1)
    widen(frecv[...])
    lax.fori_loop(0, 16 // GROUP, filter_group, 0)
    own_d.wait()
    pltpu.make_async_copy(drecv.at[pl.ds(0, 7)], drecv.at[pl.ds(0, 7)], all_recv.at[0]).wait()
    widen(drecv[...].reshape(64, 16, BLK))
    lax.fori_loop(0, 16 // GROUP, signal_group, 0)

    slot = mine * NZ + z
    own_c = []
    for side in range(2):
        lax.fori_loop(0, 16 // GROUP, inverse_group(side), 0)
        osend[side] = out32[side].reshape(64, 16, 128).astype(BF)

        own_c.append(
            to_owners(
                lambda yt, xt, zt, side=side: osend.at[side, zt * 8 + yt * NX + xt],
                crecv.at[side, slot],
                2 + side,
            )
        )

    own_q.wait()
    for copy in q_in:
        copy.wait_recv()
    for copy in own_o:
        copy.wait()

    far_h, near_h = (1 - yh) * 2, yh * 2
    p_in, y_copy = {}, {}
    for side in range(2):
        own_c[side].wait()
        from_owners(crecv.at[side], 2 + side)
        query = qrecv[:, :, 128 * side : 128 * side + 128].reshape(1024, 128).astype(F32)
        gated = (query * crecv[side].reshape(1024, 128).astype(F32)).T.astype(BF)

        def partial(h, half):
            return jnp.dot(gated, obuf[h, :, 512 * half : 512 * half + 512], preferred_element_type=F32)

        def swap(part, half, h):
            psend[side, part, half] = partial(h, half).astype(BF)
            p_in[side, part, half] = go.start(
                psend.at[side, part, half], precv.at[side, part, half], mate
            )

        swap(0, 0, far_h + 1 - core)
        total = partial(far_h + core, 0)
        swap(0, 1, far_h + 1 - core)
        for half in range(2):
            p_in[side, 0, half].wait_recv()
            ysend[side, half] = (total + precv[side, 0, half].astype(F32)).astype(BF)
            y_copy[side, half] = go.start(ysend.at[side, half], yrecv.at[side, half], across)
            if half == 0:
                total = partial(far_h + core, 1)
        for half in range(2):
            swap(1, half, near_h + 1 - core)
        for half in range(2):
            held[side, half] = partial(near_h + core, half)
    for side in range(2):
        for half in range(2):
            p_in[side, 1, half].wait_recv()
            y_copy[side, half].wait_recv()
            total = held[side, half] + precv[side, 1, half].astype(F32) + yrecv[side, half].astype(F32)
            out[pl.ds(128 * side, 128), pl.ds(512 * half, 512)] = total.astype(BF)

    go.wait_sends()
    pltpu.make_async_copy(drv.at[pl.ds(0, 7)], drv.at[pl.ds(0, 7)], all_send.at[0]).wait()
    pltpu.make_async_copy(frecv.at[pl.ds(0, 63)], frecv.at[pl.ds(0, 63)], all_send.at[1]).wait()
    for side in range(2):
        part = osend.at[side, pl.ds(0, 63)]
        pltpu.make_async_copy(part, part, all_send.at[2 + side]).wait()


def layer(act, w, taps, flt, w_out):
    any_space, vmem = pl.BlockSpec(memory_space=pl.ANY), pl.BlockSpec(memory_space=pltpu.VMEM)
    return pl.pallas_call(
        layer_kernel,
        out_shape=jax.ShapeDtypeStruct((BLK, 1024), BF),
        in_specs=[any_space] * 10,
        out_specs=vmem,
        scratch_shapes=[
            pltpu.VMEM((3, TAPS, 1024), F32),
            pltpu.VMEM((128, 128), BF),
            pltpu.VMEM((2, 64, BLK), F32),
            pltpu.VMEM((2 * BLK, 2 * BLK), BF),
            pltpu.VMEM((2 * BLK, 2 * BLK), BF),
            pltpu.VMEM((64, 256), BF),
            pltpu.VMEM((NY, NX, BLK, D), BF),
            pltpu.VMEM((NY, NX, NZ, DB, 3 * CG), BF),
            pltpu.VMEM((16, D), BF),
            pltpu.VMEM((16, 512), F32),
            pltpu.VMEM((16, 512), BF),
            pltpu.VMEM((NY, NX, 16, 512), BF),
            pltpu.VMEM((16, D), F32),
            pltpu.VMEM((8, 8, 3 * CG), F32),
            pltpu.VMEM((BLK + 8, 3 * CG), F32),
            pltpu.VMEM((1024, BLK), F32),
            pltpu.VMEM((8, NZ, 16, BLK), BF),
            pltpu.VMEM((64, 16, BLK), BF),
            pltpu.VMEM((NZ, 8, 16, BLK), BF),
            pltpu.VMEM((NZ, 8, 16, BLK), BF),
            pltpu.VMEM((8, CG, BLK), BF),
            pltpu.VMEM((8, CG, BLK), BF),
            pltpu.VMEM((2, 1024, 128), F32),
            pltpu.VMEM((2, 1024, 128), F32),
            pltpu.VMEM((16 // GROUP, 64 * GROUP, 2 * BLK), F32),
            pltpu.VMEM((16 // GROUP, 64 * GROUP, 2 * BLK), BF),
            pltpu.VMEM((2, 64, 16, 128), BF),
            pltpu.VMEM((2, 64, 16, 128), BF),
            pltpu.VMEM((4, 1024, 1024), BF),
            pltpu.VMEM((2, 2, 2, 128, 512), BF),
            pltpu.VMEM((2, 2, 2, 128, 512), BF),
            pltpu.VMEM((2, 2, 128, 512), BF),
            pltpu.VMEM((2, 2, 128, 512), BF),
            pltpu.VMEM((2, 2, 128, 512), F32),
            pltpu.SemaphoreType.DMA((16,)),
            pltpu.SemaphoreType.DMA((4,)),
            pltpu.SemaphoreType.DMA((4,)),
            pltpu.SemaphoreType.DMA((4,)),
            pltpu.SemaphoreType.DMA((N_COPIES,)),
            pltpu.SemaphoreType.DMA((N_COPIES,)),
        ],
        compiler_params=pltpu.CompilerParams(
            collective_id=0, has_side_effects=True, vmem_limit_bytes=58 * 1024 * 1024
        ),
        name="layer",
    )(act, w, taps, flt, w_out, *[jnp.asarray(table) for table in tables()])


def on_device(activations, w_in, short_taps, long_filter, w_out):
    return layer(activations, w_in, short_taps.transpose(0, 2, 1), long_filter, w_out)


def solution(mesh):
    return jax.shard_map(
        on_device,
        mesh=mesh,
        in_specs=(
            P("ctx", None),
            P(None, "ctx", "hid"),
            P(None, "hid", None),
            P("hid", "ctx"),
            P("hid", None),
        ),
        out_specs=P("ctx", "hid"),
        check_vma=False,
    )
```

```python
import math

import numpy as np
import ml_dtypes
import jax
import jax.numpy as jnp
from jax import lax
from jax.experimental import pallas as pl
from jax.experimental.pallas import tpu as pltpu
from jax.sharding import PartitionSpec as P

MESH = pl.DeviceIdType.MESH
BF = jnp.bfloat16
F32 = jnp.float32
TAPS = 3
NY, NX, NZ = 2, 4, 8
BLK = 256
D = 4096
CG = 128
DB = 64


HOOK = 0


def place():
    ctx = lax.axis_index("ctx")
    hid = lax.axis_index("hid")
    yl = lax.div(ctx, 32)
    x = lax.rem(lax.div(ctx, 8), 4)
    z = lax.rem(ctx, 8)
    return ctx, hid, yl, x, z


def at_ctx(yl, x, z):
    return {"ctx": yl * 32 + x * 8 + z}


class Copies:
    def __init__(self, send, recv):
        self.send, self.recv, self.all = send, recv, []

    def start(self, src, dst, device):
        k = len(self.all)
        copy = pltpu.make_async_remote_copy(
            src_ref=src,
            dst_ref=dst,
            send_sem=self.send.at[k],
            recv_sem=self.recv.at[k],
            device_id=device,
            device_id_type=MESH,
        )
        copy.start()
        self.all.append(copy)
        return copy

    def wait_sends(self):
        for copy in self.all:
            copy.wait_send()


def halves(table):
    high = table.astype(ml_dtypes.bfloat16)
    low = (table - high.astype(np.float64)).astype(ml_dtypes.bfloat16)
    return high, low


def tables():
    order = np.array([yl * 32 + x * 8 + z for z in range(NZ) for yl in range(NY) for x in range(NX)])
    k1 = np.arange(64) + 0.5
    angle = 2 * np.pi * np.outer(k1, np.arange(64)) / 128
    ahead = np.concatenate([np.cos(angle), -np.sin(angle)], axis=0)
    back = np.concatenate([np.cos(angle.T), -np.sin(angle.T)], axis=1) * 2.0**-14
    turn = 2 * np.pi * np.outer(k1, np.arange(BLK)) / 32768
    inner = 2 * np.pi * (np.outer(np.arange(BLK), np.arange(BLK)) % BLK) / BLK
    c, s = np.cos(inner), np.sin(inner)
    wide = np.block([[c, -s], [s, c]])
    sides = np.array([part * BLK + side * 128 + i for side in range(2) for part in range(2) for i in range(128)])
    wide = wide[sides][:, sides]
    ahead_h, ahead_l = halves(ahead[:, order])
    back_h, back_l = halves(back[order])
    wide_h, wide_l = halves(wide)
    return (
        np.concatenate([ahead_h, ahead_l], axis=1),
        np.stack([np.cos(turn), -np.sin(turn)]).astype(np.float32),
        wide_h,
        wide_l,
        np.concatenate([back_h, back_l], axis=1),
    )


N_COPIES = 160
PLANE = [(0, 0), (1, 0), (0, 1), (0, 3), (0, 2), (1, 1), (1, 3), (1, 2)]
GROUP = 4


def split(value):
    high = value.astype(BF)
    return high, (value - high.astype(F32)).astype(BF)


def layer_kernel(
    act, w, taps_in, flt, w_out, ahead_in, turn_in, wide_h_in, wide_l_in, back_in, out,
    taps, ahead, turn, wide_h, wide_l, back, abuf, wbuf, last16, packed, halo_out, halo_in, halo_act, halo_br, bs, f32buf, f16buf, frecv, drv, drecv, qry, qrecv, wide, out32, spec, prod, osend, crecv,
    obuf, psend, precv, ysend, yrecv, held, local_sem, own_sem, all_send, all_recv, send_sem, recv_sem,
):
    tables_here = (
        (taps_in, taps), (ahead_in, ahead), (turn_in, turn), (wide_h_in, wide_h), (wide_l_in, wide_l), (back_in, back)
    )
    ctx, hid, yl, x, z = place()
    core = lax.rem(hid, 2)
    yh = lax.div(hid, 2)
    mate = {"hid": hid + 1 - 2 * core}
    across = {"hid": lax.rem(hid + 2, 4)}
    xr, xl, xo = lax.rem(x + 1, NX), lax.rem(x + 3, NX), lax.rem(x + 2, NX)
    after, before = lax.rem(z + 1, NZ), lax.rem(z + NZ - 1, NZ)
    to_r, to_l = at_ctx(yl, x, after), at_ctx(yl, x, before)
    to_xr, to_xl = at_ctx(yl, xr, z), at_ctx(yl, xl, z)
    to_s = at_ctx(1 - yl, x, z)
    to_o = {"ctx": (1 - yl) * 32 + x * 8 + z, "hid": lax.rem(hid + 2, 4)}
    mine = x * NY + yl

    def rel(dy, dx):
        return lax.rem(yl + dy, NY), lax.rem(x + dx, NX)

    def columns(y, xs):
        return pl.ds(pl.multiple_of((xs * NY + y) * CG, CG), CG)

    own_w = [
        pltpu.make_async_copy(
            w.at[j, :, columns(yl, x)], wbuf.at[yl, x, z, :, pl.ds(j * CG, CG)], local_sem.at[13 + j]
        )
        for j in range(3)
    ]
    own_a = pltpu.make_async_copy(act, abuf.at[yl, x], local_sem.at[1])
    tail = pltpu.make_async_copy(act.at[pl.ds(BLK - 16, 16)], last16, local_sem.at[0])
    for copy in own_w + [tail, own_a]:
        copy.start()

    barrier = pltpu.get_barrier_semaphore()
    peers = [mate, across, to_o] + [at_ctx(*rel(dy, dx), z) for dy, dx in PLANE[1:]]
    for dy, dx in PLANE:
        peers += [at_ctx(*rel(dy, dx), after), at_ctx(*rel(dy, dx), before)]
    for peer in peers:
        pl.semaphore_signal(barrier, inc=1, device_id=peer, device_id_type=MESH)
    pl.semaphore_wait(barrier, len(peers))

    go = Copies(send_sem, recv_sem)
    first = {}
    for dy, dx in PLANE[1:]:
        yt, xt = rel(dy, dx)
        first[dy, (NX - dx) % NX] = [
            go.start(
                w.at[j, :, columns(yt, xt)], wbuf.at[yl, x, z, :, pl.ds(j * CG, CG)], at_ctx(yt, xt, z)
            )
            for j in range(3)
        ]

    def a_slot(y, block, part, first_row=0, count=64):
        return abuf.at[y, block, pl.ds(pl.multiple_of(core * 128 + part * 64 + first_row, 16), count)]

    def a_send(part, to):
        return go.start(
            act.at[pl.ds(pl.multiple_of(core * 128 + part * 64, 64), 64)], a_slot(yl, x, part), to
        )

    y_in, mates = {}, {}

    def y_send(block, dx, part, count=32):
        for half, to in ((0, to_s), (1, to_o)):
            piece = a_slot(yl, block, part, half * count, count)
            y_in[dx, part, half] = go.start(piece, piece, to)

    def mate_own(block, dx, part):
        mates[0, dx, part] = go.start(a_slot(yl, block, part), a_slot(yl, block, part), mate)

    def mate_other(block, dx, part):
        y_in[dx, part, 0].wait_recv()
        y_in[dx, part, 1].wait_recv()
        if dx == 2:
            far_other[part].wait_recv()
        mates[1, dx, part] = go.start(a_slot(1 - yl, block, part), a_slot(1 - yl, block, part), mate)

    near = [a_send(0, to_xr), a_send(1, to_xl)]
    for part in range(2):
        for half, to in ((0, to_s), (1, to_o)):
            begin = pl.multiple_of(core * 128 + part * 64 + half * 32, 32)
            y_in[0, part, half] = go.start(
                act.at[pl.ds(begin, 32)], a_slot(yl, x, part, half * 32, 32), to
            )

    def send(unit, zs, to):
        yu, xu = rel(*unit)
        part = wbuf.at[yu, xu, zs]
        return go.start(part, part, to)

    from_l, from_r = {}, {}

    def send_own(unit):
        from_l[unit, 1] = send(unit, z, to_r)
        from_r[unit, 1] = send(unit, z, to_l)

    loads = [pltpu.make_async_copy(flt, f32buf, local_sem.at[2])]
    for k, (table, kept) in enumerate(tables_here):
        loads.append(pltpu.make_async_copy(table, kept, local_sem.at[7 + k]))
    own_o = [
        pltpu.make_async_copy(w_out.at[:, pl.ds(1024 * h, 1024)], obuf.at[h], local_sem.at[3 + h])
        for h in range(4)
    ]
    for copy in loads:
        copy.start()
    for copy in own_w:
        copy.wait()
    send_own((0, 0))

    tail.wait()
    rows = last16[...].astype(F32)
    for k in range(8):
        packed[pl.ds(2 * k, 2), :] = rows[14:16, 512 * k : 512 * k + 512]
    halo_out[...] = packed[...].astype(BF)
    halos = []
    x_next = lax.rem(x + lax.div(z + 1, NZ), NX)
    y_next = lax.rem(yl + lax.div(x * NZ + z + 1, NX * NZ), NY)
    for dy, dx in PLANE:
        halos.append(go.start(halo_out, halo_in.at[y_next, x_next], at_ctx(*rel(dy, dx), after)))

    for unit in PLANE[1:]:
        for copy in first[unit]:
            copy.wait_recv()
        send_own(unit)

    for copy in loads:
        copy.wait()
    f16buf[...] = f32buf[...].astype(BF).reshape(8, NZ, 16, BLK)

    def relay(step):
        zl, zr = lax.rem(z + NZ - step, NZ), lax.rem(z + step, NZ)
        for k, unit in enumerate(PLANE):
            from_l[unit, step].wait_recv()
            if step < 3 or k % 2 == 0:
                from_l[unit, step + 1] = send(unit, zl, to_r)
            from_r[unit, step].wait_recv()
            if step < 3 or k % 2 == 1:
                from_r[unit, step + 1] = send(unit, zr, to_l)
            if step == 1 and k == 4:
                near.extend([a_send(1, to_xr), a_send(0, to_xl)])
            if k == HOOK and step in hooks:
                hooks[step]()

    def first_halves():
        near[0].wait_recv()
        y_send(xl, 3, 0)
        mate_own(xl, 3, 0)
        near[1].wait_recv()
        y_send(xr, 1, 1)
        mate_own(xr, 1, 1)
        far.append(go.start(a_slot(yl, xl, 0), a_slot(yl, xl, 0), to_xr))
        far.append(go.start(a_slot(yl, xr, 1), a_slot(yl, xr, 1), to_xl))

    def second_halves():
        near[2].wait_recv()
        y_send(xl, 3, 1)
        mate_own(xl, 3, 1)
        near[3].wait_recv()
        y_send(xr, 1, 0)
        mate_own(xr, 1, 0)

    far, far_other, hooks = [], [], {2: first_halves, 3: second_halves}
    own_a.wait()
    relay(1)
    for copy in own_o:
        copy.start()
    relay(2)
    mate_other(x, 0, 0)
    mate_other(x, 0, 1)
    for copy in halos:
        copy.wait_recv()
    for y in range(NY):
        for xs in range(NX):
            got = halo_in[y, xs].astype(F32)
            for k in range(8):
                halo_act[pl.ds(2 * (y * NX + xs), 2), pl.ds(512 * k, 512)] = got[2 * k : 2 * k + 2]
    relay(3)
    mate_other(xl, 3, 0)
    mate_other(xr, 1, 1)
    for block, part, to in ((xl, 0, to_xr), (xr, 1, to_xl)):
        piece = a_slot(1 - yl, block, part, 32, 32)
        far_other.append(go.start(piece, piece, to))

    def to_owners(src, dst, sem):
        def one(t, carry):
            c = lax.rem(ctx + t, 64)
            yt, xt, zt = lax.div(c, 32), lax.rem(lax.div(c, 8), 4), lax.rem(c, 8)
            pltpu.make_async_remote_copy(
                src_ref=src(yt, xt, zt),
                dst_ref=dst,
                send_sem=all_send.at[sem],
                recv_sem=all_recv.at[sem],
                device_id={"ctx": c},
                device_id_type=MESH,
            ).start()
            return carry

        lax.fori_loop(1, 64, one, 0)
        own = pltpu.make_async_copy(src(yl, x, z), dst, own_sem.at[sem])
        own.start()
        return own

    def from_owners(dst, sem):
        arrived = dst.at[pl.ds(0, 63)]
        pltpu.make_async_copy(arrived, arrived, all_recv.at[sem]).wait()

    here = z * 8 + yl * NX + x
    own_f = to_owners(lambda yt, xt, zt: f16buf.at[xt * NY + yt, zt], frecv.at[here], 1)
    for k, unit in enumerate(PLANE):
        (from_l if k % 2 == 0 else from_r)[unit, 4].wait_recv()
    def await_mates(keys):
        for key in keys:
            for part in range(2):
                mates[(*key, part)].wait_recv()

    rims = jnp.dot(
        halo_act[...].astype(BF), wbuf[...].reshape(D, 3 * CG), preferred_element_type=F32
    ).astype(BF).astype(F32)
    halo_br[...] = jnp.zeros_like(halo_br)
    for b in range(8):
        halo_br[b, pl.ds(6, 2)] = rims[2 * b : 2 * b + 2]

    def block(yb, xb):
        at = yb * NX + xb
        keep = jnp.where(yb * 32 + xb * 8 + z == 0, 0.0, 1.0).astype(F32)
        bs[pl.ds(8, BLK)] = (
            jnp.dot(abuf[yb, xb], wbuf[...].reshape(D, 3 * CG), preferred_element_type=F32).astype(BF).astype(F32)
        )
        bs[pl.ds(0, 8)] = halo_br[at] * keep
        filtered = []
        for j in range(3):
            lanes = slice(j * CG, j * CG + CG)
            total = taps[j, pl.ds(0, 1), columns(yl, x)] * bs[pl.ds(8, BLK), lanes]
            for k in range(1, TAPS):
                total = total + taps[j, pl.ds(k, 1), columns(yl, x)] * bs[pl.ds(8 - k, BLK), lanes]
            filtered.append(total)
        drv[:, at] = (filtered[0] * filtered[2]).T.astype(BF).reshape(NZ, 16, BLK)

        def one(t, carry):
            zt = lax.rem(z + t, NZ)
            pltpu.make_async_remote_copy(
                src_ref=drv.at[zt, at],
                dst_ref=drecv.at[z, at],
                send_sem=all_send.at[0],
                recv_sem=all_recv.at[0],
                device_id=at_ctx(yl, x, zt),
                device_id_type=MESH,
            ).start()
            return carry

        lax.fori_loop(1, NZ, one, 0)
        qry[at] = filtered[1].T.astype(BF)

    def early(t, carry):
        block(lax.rem(yl + lax.div(t, 3), NY), lax.rem(x + t + lax.div(t, 2), NX))
        return carry

    def middle(t, carry):
        block(1 - yl, lax.rem(x + 1 + 2 * t, NX))
        return carry

    await_mates([(0, 1), (0, 3), (1, 0)])
    lax.fori_loop(0, 2, early, 0)
    for part in range(2):
        far[part].wait_recv()
        y_send(xo, 2, part, 16)
        mate_own(xo, 2, part)
    lax.fori_loop(2, 4, early, 0)


    mate_other(xl, 3, 1)
    mate_other(xr, 1, 0)
    await_mates([(1, 1), (1, 3), (0, 2)])
    lax.fori_loop(0, 2, middle, 0)
    block(yl, xo)
    mate_other(xo, 2, 0)
    mate_other(xo, 2, 1)
    await_mates([(1, 2)])
    block(1 - yl, xo)

    own_d = pltpu.make_async_copy(drv.at[z], drecv.at[z], own_sem.at[0])
    own_d.start()
    own_q = pltpu.make_async_copy(qry.at[yl * NX + x], qrecv.at[mine], local_sem.at[0])
    own_q.start()
    q_in = []
    for dy, dx in PLANE[1:]:
        yt, xt = rel(dy, dx)
        q_in.append(go.start(qry.at[yt * NX + xt], qrecv.at[mine], at_ctx(yt, xt, z)))

    def inner(high, columns):
        return jnp.dot(high, wide_h[:, columns], preferred_element_type=F32)

    def widen(source):
        for side in range(2):
            half = source[:, :, 128 * side : 128 * side + 128]
            wide[side] = half.astype(F32).reshape(1024, 128)

    def turned(first):
        parts = []
        for i in range(GROUP):
            rows = jnp.concatenate(
                [wide[side, pl.ds(first + i, 64, stride=16), :] for side in range(2)], axis=1
            ).astype(BF)
            both = jnp.dot(ahead[...], jnp.concatenate([rows, rows], axis=0), preferred_element_type=F32)
            pieces = []
            for side in range(2):
                at = slice(128 * side, 128 * side + 128)
                re, im, tr, ti = both[:64, at], both[64:, at], turn[0, :, at], turn[1, :, at]
                pieces += [re * tr - im * ti, re * ti + im * tr]
            parts.append(jnp.concatenate(pieces, axis=1))
        return jnp.concatenate(parts, axis=0)

    def filter_group(g, carry):
        high, low = split(turned(g * GROUP))
        spec[g] = (
            inner(high, slice(None))
            + inner(low, slice(None))
            + jnp.dot(high, wide_l[...], preferred_element_type=F32)
        )
        return carry

    def signal_group(g, carry):
        s = inner(turned(g * GROUP).astype(BF), slice(None))
        for side in range(2):
            re, im = slice(256 * side, 256 * side + 128), slice(256 * side + 128, 256 * side + 256)
            sr, si, hr, hi = s[:, re], s[:, im], spec[g, :, re], spec[g, :, im]
            prod[g, :, re] = (sr * hr - si * hi).astype(BF)
            prod[g, :, im] = -(sr * hi + si * hr).astype(BF)
        return carry

    def inverse_group(side):
        at = slice(128 * side, 128 * side + 128)

        def one(g, carry):
            v = inner(prod[g], slice(256 * side, 256 * side + 256))
            for i in range(0, GROUP, 2):
                pair = []
                for c in (i, i + 1):
                    re, im = v[64 * c : 64 * c + 64, :128], -v[64 * c : 64 * c + 64, 128:]
                    tr, ti = turn[0, :, at], turn[1, :, at]
                    pair.append(jnp.concatenate([re * tr + im * ti, im * tr - re * ti], axis=0))
                high = jnp.concatenate(pair, axis=1).astype(BF)
                y = jnp.dot(back[...], jnp.concatenate([high, high], axis=0), preferred_element_type=F32)
                out32[side, pl.ds(g * GROUP + i, 64, stride=16), :] = y[:, :128]
                out32[side, pl.ds(g * GROUP + i + 1, 64, stride=16), :] = y[:, 128:]
            return carry

        return one

    own_f.wait()
    from_owners(frecv, 1)
    widen(frecv[...])
    lax.fori_loop(0, 16 // GROUP, filter_group, 0)
    own_d.wait()
    pltpu.make_async_copy(drecv.at[pl.ds(0, 7)], drecv.at[pl.ds(0, 7)], all_recv.at[0]).wait()
    widen(drecv[...].reshape(64, 16, BLK))
    lax.fori_loop(0, 16 // GROUP, signal_group, 0)

    slot = mine * NZ + z
    own_c = []
    for side in range(2):
        lax.fori_loop(0, 16 // GROUP, inverse_group(side), 0)
        osend[side] = out32[side].reshape(64, 16, 128).astype(BF)

        own_c.append(
            to_owners(
                lambda yt, xt, zt, side=side: osend.at[side, zt * 8 + yt * NX + xt],
                crecv.at[side, slot],
                2 + side,
            )
        )

    own_q.wait()
    for copy in q_in:
        copy.wait_recv()
    for copy in own_o:
        copy.wait()

    far_h, near_h = (1 - yh) * 2, yh * 2
    p_in, y_copy = {}, {}
    for side in range(2):
        own_c[side].wait()
        from_owners(crecv.at[side], 2 + side)
        query = qrecv[:, :, 128 * side : 128 * side + 128].reshape(1024, 128).astype(F32)
        gated = (query * crecv[side].reshape(1024, 128).astype(F32)).T.astype(BF)

        def partial(h, half):
            return jnp.dot(gated, obuf[h, :, 512 * half : 512 * half + 512], preferred_element_type=F32)

        def swap(part, half, h):
            psend[side, part, half] = partial(h, half).astype(BF)
            p_in[side, part, half] = go.start(
                psend.at[side, part, half], precv.at[side, part, half], mate
            )

        swap(0, 0, far_h + 1 - core)
        total = partial(far_h + core, 0)
        swap(0, 1, far_h + 1 - core)
        for half in range(2):
            p_in[side, 0, half].wait_recv()
            ysend[side, half] = (total + precv[side, 0, half].astype(F32)).astype(BF)
            y_copy[side, half] = go.start(ysend.at[side, half], yrecv.at[side, half], across)
            if half == 0:
                total = partial(far_h + core, 1)
        for half in range(2):
            swap(1, half, near_h + 1 - core)
        for half in range(2):
            held[side, half] = partial(near_h + core, half)
    for side in range(2):
        for half in range(2):
            p_in[side, 1, half].wait_recv()
            y_copy[side, half].wait_recv()
            total = held[side, half] + precv[side, 1, half].astype(F32) + yrecv[side, half].astype(F32)
            out[pl.ds(128 * side, 128), pl.ds(512 * half, 512)] = total.astype(BF)

    go.wait_sends()
    pltpu.make_async_copy(drv.at[pl.ds(0, 7)], drv.at[pl.ds(0, 7)], all_send.at[0]).wait()
    pltpu.make_async_copy(frecv.at[pl.ds(0, 63)], frecv.at[pl.ds(0, 63)], all_send.at[1]).wait()
    for side in range(2):
        part = osend.at[side, pl.ds(0, 63)]
        pltpu.make_async_copy(part, part, all_send.at[2 + side]).wait()


def layer(act, w, taps, flt, w_out):
    any_space, vmem = pl.BlockSpec(memory_space=pl.ANY), pl.BlockSpec(memory_space=pltpu.VMEM)
    return pl.pallas_call(
        layer_kernel,
        out_shape=jax.ShapeDtypeStruct((BLK, 1024), BF),
        in_specs=[any_space] * 10,
        out_specs=vmem,
        scratch_shapes=[
            pltpu.VMEM((3, TAPS, 1024), F32),
            pltpu.VMEM((128, 128), BF),
            pltpu.VMEM((2, 64, BLK), F32),
            pltpu.VMEM((2 * BLK, 2 * BLK), BF),
            pltpu.VMEM((2 * BLK, 2 * BLK), BF),
            pltpu.VMEM((64, 256), BF),
            pltpu.VMEM((NY, NX, BLK, D), BF),
            pltpu.VMEM((NY, NX, NZ, DB, 3 * CG), BF),
            pltpu.VMEM((16, D), BF),
            pltpu.VMEM((16, 512), F32),
            pltpu.VMEM((16, 512), BF),
            pltpu.VMEM((NY, NX, 16, 512), BF),
            pltpu.VMEM((16, D), F32),
            pltpu.VMEM((8, 8, 3 * CG), F32),
            pltpu.VMEM((BLK + 8, 3 * CG), F32),
            pltpu.VMEM((1024, BLK), F32),
            pltpu.VMEM((8, NZ, 16, BLK), BF),
            pltpu.VMEM((64, 16, BLK), BF),
            pltpu.VMEM((NZ, 8, 16, BLK), BF),
            pltpu.VMEM((NZ, 8, 16, BLK), BF),
            pltpu.VMEM((8, CG, BLK), BF),
            pltpu.VMEM((8, CG, BLK), BF),
            pltpu.VMEM((2, 1024, 128), F32),
            pltpu.VMEM((2, 1024, 128), F32),
            pltpu.VMEM((16 // GROUP, 64 * GROUP, 2 * BLK), F32),
            pltpu.VMEM((16 // GROUP, 64 * GROUP, 2 * BLK), BF),
            pltpu.VMEM((2, 64, 16, 128), BF),
            pltpu.VMEM((2, 64, 16, 128), BF),
            pltpu.VMEM((4, 1024, 1024), BF),
            pltpu.VMEM((2, 2, 2, 128, 512), BF),
            pltpu.VMEM((2, 2, 2, 128, 512), BF),
            pltpu.VMEM((2, 2, 128, 512), BF),
            pltpu.VMEM((2, 2, 128, 512), BF),
            pltpu.VMEM((2, 2, 128, 512), F32),
            pltpu.SemaphoreType.DMA((16,)),
            pltpu.SemaphoreType.DMA((4,)),
            pltpu.SemaphoreType.DMA((4,)),
            pltpu.SemaphoreType.DMA((4,)),
            pltpu.SemaphoreType.DMA((N_COPIES,)),
            pltpu.SemaphoreType.DMA((N_COPIES,)),
        ],
        compiler_params=pltpu.CompilerParams(
            collective_id=0, has_side_effects=True, vmem_limit_bytes=58 * 1024 * 1024
        ),
        name="layer",
    )(act, w, taps, flt, w_out, *[jnp.asarray(table) for table in tables()])


def on_device(activations, w_in, short_taps, long_filter, w_out):
    return layer(activations, w_in, short_taps.transpose(0, 2, 1), long_filter, w_out)


def solution(mesh):
    return jax.shard_map(
        on_device,
        mesh=mesh,
        in_specs=(
            P("ctx", None),
            P(None, "ctx", "hid"),
            P(None, "hid", None),
            P("hid", "ctx"),
            P("hid", None),
        ),
        out_specs=P("ctx", "hid"),
        check_vma=False,
    )
```

```python
import math

import numpy as np
import ml_dtypes
import jax
import jax.numpy as jnp
from jax import lax
from jax.experimental import pallas as pl
from jax.experimental.pallas import tpu as pltpu
from jax.sharding import PartitionSpec as P

MESH = pl.DeviceIdType.MESH
BF = jnp.bfloat16
F32 = jnp.float32
TAPS = 3
NY, NX, NZ = 2, 4, 8
BLK = 256
D = 4096
CG = 128
DB = 64


HOOK = 0


def place():
    ctx = lax.axis_index("ctx")
    hid = lax.axis_index("hid")
    yl = lax.div(ctx, 32)
    x = lax.rem(lax.div(ctx, 8), 4)
    z = lax.rem(ctx, 8)
    return ctx, hid, yl, x, z


def at_ctx(yl, x, z):
    return {"ctx": yl * 32 + x * 8 + z}


class Copies:
    def __init__(self, send, recv):
        self.send, self.recv, self.all = send, recv, []

    def start(self, src, dst, device):
        k = len(self.all)
        copy = pltpu.make_async_remote_copy(
            src_ref=src,
            dst_ref=dst,
            send_sem=self.send.at[k],
            recv_sem=self.recv.at[k],
            device_id=device,
            device_id_type=MESH,
        )
        copy.start()
        self.all.append(copy)
        return copy

    def wait_sends(self):
        for copy in self.all:
            copy.wait_send()


def halves(table):
    high = table.astype(ml_dtypes.bfloat16)
    low = (table - high.astype(np.float64)).astype(ml_dtypes.bfloat16)
    return high, low


def tables():
    order = np.array([yl * 32 + x * 8 + z for z in range(NZ) for yl in range(NY) for x in range(NX)])
    k1 = np.arange(64) + 0.5
    angle = 2 * np.pi * np.outer(k1, np.arange(64)) / 128
    ahead = np.concatenate([np.cos(angle), -np.sin(angle)], axis=0)
    back = np.concatenate([np.cos(angle.T), -np.sin(angle.T)], axis=1) * 2.0**-14
    turn = 2 * np.pi * np.outer(k1, np.arange(BLK)) / 32768
    inner = 2 * np.pi * (np.outer(np.arange(BLK), np.arange(BLK)) % BLK) / BLK
    c, s = np.cos(inner), np.sin(inner)
    wide = np.block([[c, -s], [s, c]])
    sides = np.array([part * BLK + side * 128 + i for side in range(2) for part in range(2) for i in range(128)])
    wide = wide[sides][:, sides]
    ahead_h, ahead_l = halves(ahead[:, order])
    back_h, back_l = halves(back[order])
    wide_h, _ = halves(wide)
    return (
        np.concatenate([ahead_h, ahead_l], axis=1),
        np.stack([np.cos(turn), -np.sin(turn)]).astype(np.float32),
        wide_h,
        np.concatenate([back_h, back_l], axis=1),
    )


N_COPIES = 160
PLANE = [(0, 0), (1, 0), (0, 1), (0, 3), (0, 2), (1, 1), (1, 3), (1, 2)]
GROUP = 4


def split(value):
    high = value.astype(BF)
    return high, (value - high.astype(F32)).astype(BF)


def layer_kernel(
    act, w, taps_in, flt, w_out, ahead_in, turn_in, wide_h_in, back_in, out,
    taps, ahead, turn, wide_h, back, abuf, wbuf, last16, packed, halo_out, halo_in, halo_act, halo_br, bs, f32buf, f16buf, frecv, drv, drecv, qry, qrecv, wide, out32, spec, prod, osend, crecv,
    obuf, psend, precv, ysend, yrecv, held, local_sem, own_sem, all_send, all_recv, send_sem, recv_sem,
):
    tables_here = (
        (taps_in, taps), (ahead_in, ahead), (turn_in, turn), (wide_h_in, wide_h), (back_in, back)
    )
    ctx, hid, yl, x, z = place()
    core = lax.rem(hid, 2)
    yh = lax.div(hid, 2)
    mate = {"hid": hid + 1 - 2 * core}
    across = {"hid": lax.rem(hid + 2, 4)}
    xr, xl, xo = lax.rem(x + 1, NX), lax.rem(x + 3, NX), lax.rem(x + 2, NX)
    after, before = lax.rem(z + 1, NZ), lax.rem(z + NZ - 1, NZ)
    to_r, to_l = at_ctx(yl, x, after), at_ctx(yl, x, before)
    to_xr, to_xl = at_ctx(yl, xr, z), at_ctx(yl, xl, z)
    to_s = at_ctx(1 - yl, x, z)
    to_o = {"ctx": (1 - yl) * 32 + x * 8 + z, "hid": lax.rem(hid + 2, 4)}
    mine = x * NY + yl

    def rel(dy, dx):
        return lax.rem(yl + dy, NY), lax.rem(x + dx, NX)

    def columns(y, xs):
        return pl.ds(pl.multiple_of((xs * NY + y) * CG, CG), CG)

    own_w = [
        pltpu.make_async_copy(
            w.at[j, :, columns(yl, x)], wbuf.at[yl, x, z, :, pl.ds(j * CG, CG)], local_sem.at[13 + j]
        )
        for j in range(3)
    ]
    own_a = pltpu.make_async_copy(act, abuf.at[yl, x], local_sem.at[1])
    tail = pltpu.make_async_copy(act.at[pl.ds(BLK - 16, 16)], last16, local_sem.at[0])
    for copy in own_w + [tail, own_a]:
        copy.start()

    barrier = pltpu.get_barrier_semaphore()
    peers = [mate, across, to_o] + [at_ctx(*rel(dy, dx), z) for dy, dx in PLANE[1:]]
    for dy, dx in PLANE:
        peers += [at_ctx(*rel(dy, dx), after), at_ctx(*rel(dy, dx), before)]
    for peer in peers:
        pl.semaphore_signal(barrier, inc=1, device_id=peer, device_id_type=MESH)
    pl.semaphore_wait(barrier, len(peers))

    go = Copies(send_sem, recv_sem)
    first = {}
    for dy, dx in PLANE[1:]:
        yt, xt = rel(dy, dx)
        first[dy, (NX - dx) % NX] = [
            go.start(
                w.at[j, :, columns(yt, xt)], wbuf.at[yl, x, z, :, pl.ds(j * CG, CG)], at_ctx(yt, xt, z)
            )
            for j in range(3)
        ]

    def a_slot(y, block, part, first_row=0, count=64):
        return abuf.at[y, block, pl.ds(pl.multiple_of(core * 128 + part * 64 + first_row, 16), count)]

    def a_send(part, to):
        return go.start(
            act.at[pl.ds(pl.multiple_of(core * 128 + part * 64, 64), 64)], a_slot(yl, x, part), to
        )

    y_in, mates = {}, {}

    def y_send(block, dx, part, count=32):
        for half, to in ((0, to_s), (1, to_o)):
            piece = a_slot(yl, block, part, half * count, count)
            y_in[dx, part, half] = go.start(piece, piece, to)

    def mate_own(block, dx, part):
        mates[0, dx, part] = go.start(a_slot(yl, block, part), a_slot(yl, block, part), mate)

    def mate_other(block, dx, part):
        y_in[dx, part, 0].wait_recv()
        y_in[dx, part, 1].wait_recv()
        if dx == 2:
            far_other[part].wait_recv()
        mates[1, dx, part] = go.start(a_slot(1 - yl, block, part), a_slot(1 - yl, block, part), mate)

    near = [a_send(0, to_xr), a_send(1, to_xl)]
    for part in range(2):
        for half, to in ((0, to_s), (1, to_o)):
            begin = pl.multiple_of(core * 128 + part * 64 + half * 32, 32)
            y_in[0, part, half] = go.start(
                act.at[pl.ds(begin, 32)], a_slot(yl, x, part, half * 32, 32), to
            )

    def send(unit, zs, to):
        yu, xu = rel(*unit)
        part = wbuf.at[yu, xu, zs]
        return go.start(part, part, to)

    from_l, from_r = {}, {}

    def send_own(unit):
        from_l[unit, 1] = send(unit, z, to_r)
        from_r[unit, 1] = send(unit, z, to_l)

    loads = [pltpu.make_async_copy(flt, f32buf, local_sem.at[2])]
    for k, (table, kept) in enumerate(tables_here):
        loads.append(pltpu.make_async_copy(table, kept, local_sem.at[7 + k]))
    own_o = [
        pltpu.make_async_copy(w_out.at[:, pl.ds(1024 * h, 1024)], obuf.at[h], local_sem.at[3 + h])
        for h in range(4)
    ]
    for copy in loads:
        copy.start()
    for copy in own_w:
        copy.wait()
    send_own((0, 0))

    tail.wait()
    rows = last16[...].astype(F32)
    for k in range(8):
        packed[pl.ds(2 * k, 2), :] = rows[14:16, 512 * k : 512 * k + 512]
    halo_out[...] = packed[...].astype(BF)
    halos = []
    x_next = lax.rem(x + lax.div(z + 1, NZ), NX)
    y_next = lax.rem(yl + lax.div(x * NZ + z + 1, NX * NZ), NY)
    for dy, dx in PLANE:
        halos.append(go.start(halo_out, halo_in.at[y_next, x_next], at_ctx(*rel(dy, dx), after)))

    for unit in PLANE[1:]:
        for copy in first[unit]:
            copy.wait_recv()
        send_own(unit)

    for copy in loads:
        copy.wait()
    f16buf[...] = f32buf[...].astype(BF).reshape(8, NZ, 16, BLK)

    def relay(step):
        zl, zr = lax.rem(z + NZ - step, NZ), lax.rem(z + step, NZ)
        for k, unit in enumerate(PLANE):
            from_l[unit, step].wait_recv()
            if step < 3 or k % 2 == 0:
                from_l[unit, step + 1] = send(unit, zl, to_r)
            from_r[unit, step].wait_recv()
            if step < 3 or k % 2 == 1:
                from_r[unit, step + 1] = send(unit, zr, to_l)
            if step == 1 and k == 1:
                near.extend([a_send(1, to_xr), a_send(0, to_xl)])
            if k == HOOK and step in hooks:
                hooks[step]()

    def first_halves():
        near[0].wait_recv()
        y_send(xl, 3, 0)
        mate_own(xl, 3, 0)
        near[1].wait_recv()
        y_send(xr, 1, 1)
        mate_own(xr, 1, 1)
        far.append(go.start(a_slot(yl, xl, 0), a_slot(yl, xl, 0), to_xr))
        far.append(go.start(a_slot(yl, xr, 1), a_slot(yl, xr, 1), to_xl))

    def second_halves():
        near[2].wait_recv()
        y_send(xl, 3, 1)
        mate_own(xl, 3, 1)
        near[3].wait_recv()
        y_send(xr, 1, 0)
        mate_own(xr, 1, 0)

    far, far_other, hooks = [], [], {2: first_halves, 3: second_halves}
    own_a.wait()
    relay(1)
    for copy in own_o:
        copy.start()
    relay(2)
    mate_other(x, 0, 0)
    mate_other(x, 0, 1)
    relay(3)
    mate_other(xl, 3, 0)
    mate_other(xr, 1, 1)
    for block, part, to in ((xl, 0, to_xr), (xr, 1, to_xl)):
        piece = a_slot(1 - yl, block, part, 32, 32)
        far_other.append(go.start(piece, piece, to))

    def to_owners(src, dst, sem):
        def one(t, carry):
            c = lax.rem(ctx + t, 64)
            yt, xt, zt = lax.div(c, 32), lax.rem(lax.div(c, 8), 4), lax.rem(c, 8)
            pltpu.make_async_remote_copy(
                src_ref=src(yt, xt, zt),
                dst_ref=dst,
                send_sem=all_send.at[sem],
                recv_sem=all_recv.at[sem],
                device_id={"ctx": c},
                device_id_type=MESH,
            ).start()
            return carry

        lax.fori_loop(1, 64, one, 0)
        own = pltpu.make_async_copy(src(yl, x, z), dst, own_sem.at[sem])
        own.start()
        return own

    def from_owners(dst, sem):
        arrived = dst.at[pl.ds(0, 63)]
        pltpu.make_async_copy(arrived, arrived, all_recv.at[sem]).wait()

    here = z * 8 + yl * NX + x
    own_f = to_owners(lambda yt, xt, zt: f16buf.at[xt * NY + yt, zt], frecv.at[here], 1)
    for k, unit in enumerate(PLANE):
        (from_l if k % 2 == 0 else from_r)[unit, 4].wait_recv()
    for copy in halos:
        copy.wait_recv()
    for y in range(NY):
        for xs in range(NX):
            got = halo_in[y, xs].astype(F32)
            for k in range(8):
                halo_act[pl.ds(2 * (y * NX + xs), 2), pl.ds(512 * k, 512)] = got[2 * k : 2 * k + 2]

    def await_mates(keys):
        for key in keys:
            for part in range(2):
                mates[(*key, part)].wait_recv()

    rims = jnp.dot(
        halo_act[...].astype(BF), wbuf[...].reshape(D, 3 * CG), preferred_element_type=F32
    ).astype(BF).astype(F32)
    halo_br[...] = jnp.zeros_like(halo_br)
    for b in range(8):
        halo_br[b, pl.ds(6, 2)] = rims[2 * b : 2 * b + 2]

    def block(yb, xb):
        at = yb * NX + xb
        keep = jnp.where(yb * 32 + xb * 8 + z == 0, 0.0, 1.0).astype(F32)
        bs[pl.ds(8, BLK)] = (
            jnp.dot(abuf[yb, xb], wbuf[...].reshape(D, 3 * CG), preferred_element_type=F32).astype(BF).astype(F32)
        )
        bs[pl.ds(0, 8)] = halo_br[at] * keep
        filtered = []
        for j in range(3):
            lanes = slice(j * CG, j * CG + CG)
            total = taps[j, pl.ds(0, 1), columns(yl, x)] * bs[pl.ds(8, BLK), lanes]
            for k in range(1, TAPS):
                total = total + taps[j, pl.ds(k, 1), columns(yl, x)] * bs[pl.ds(8 - k, BLK), lanes]
            filtered.append(total)
        drv[:, at] = (filtered[0] * filtered[2]).T.astype(BF).reshape(NZ, 16, BLK)

        def one(t, carry):
            zt = lax.rem(z + t, NZ)
            pltpu.make_async_remote_copy(
                src_ref=drv.at[zt, at],
                dst_ref=drecv.at[z, at],
                send_sem=all_send.at[0],
                recv_sem=all_recv.at[0],
                device_id=at_ctx(yl, x, zt),
                device_id_type=MESH,
            ).start()
            return carry

        lax.fori_loop(1, NZ, one, 0)
        qry[at] = filtered[1].T.astype(BF)

    def early(t, carry):
        block(lax.rem(yl + lax.div(t, 3), NY), lax.rem(x + t + lax.div(t, 2), NX))
        return carry

    def middle(t, carry):
        block(1 - yl, lax.rem(x + 1 + 2 * t, NX))
        return carry

    await_mates([(0, 1), (0, 3), (1, 0)])
    lax.fori_loop(0, 3, early, 0)
    for part in range(2):
        far[part].wait_recv()
        y_send(xo, 2, part, 16)
        mate_own(xo, 2, part)
    lax.fori_loop(3, 4, early, 0)


    mate_other(xl, 3, 1)
    mate_other(xr, 1, 0)
    await_mates([(1, 1), (1, 3), (0, 2)])
    lax.fori_loop(0, 2, middle, 0)
    block(yl, xo)
    mate_other(xo, 2, 0)
    mate_other(xo, 2, 1)
    await_mates([(1, 2)])
    block(1 - yl, xo)

    own_d = pltpu.make_async_copy(drv.at[z], drecv.at[z], own_sem.at[0])
    own_d.start()
    own_q = pltpu.make_async_copy(qry.at[yl * NX + x], qrecv.at[mine], local_sem.at[0])
    own_q.start()
    q_in = []
    for dy, dx in PLANE[1:]:
        yt, xt = rel(dy, dx)
        q_in.append(go.start(qry.at[yt * NX + xt], qrecv.at[mine], at_ctx(yt, xt, z)))

    def inner(high, columns):
        return jnp.dot(high, wide_h[:, columns], preferred_element_type=F32)

    def widen(source):
        for side in range(2):
            half = source[:, :, 128 * side : 128 * side + 128]
            wide[side] = half.astype(F32).reshape(1024, 128)

    def turned(first):
        parts = []
        for i in range(GROUP):
            rows = jnp.concatenate(
                [wide[side, pl.ds(first + i, 64, stride=16), :] for side in range(2)], axis=1
            ).astype(BF)
            both = jnp.dot(ahead[...], jnp.concatenate([rows, rows], axis=0), preferred_element_type=F32)
            pieces = []
            for side in range(2):
                at = slice(128 * side, 128 * side + 128)
                re, im, tr, ti = both[:64, at], both[64:, at], turn[0, :, at], turn[1, :, at]
                pieces += [re * tr - im * ti, re * ti + im * tr]
            parts.append(jnp.concatenate(pieces, axis=1))
        return jnp.concatenate(parts, axis=0)

    def filter_group(g, carry):
        spec[g] = inner(turned(g * GROUP).astype(BF), slice(None))
        return carry

    def signal_group(g, carry):
        s = inner(turned(g * GROUP).astype(BF), slice(None))
        for side in range(2):
            re, im = slice(256 * side, 256 * side + 128), slice(256 * side + 128, 256 * side + 256)
            sr, si, hr, hi = s[:, re], s[:, im], spec[g, :, re], spec[g, :, im]
            prod[g, :, re] = (sr * hr - si * hi).astype(BF)
            prod[g, :, im] = -(sr * hi + si * hr).astype(BF)
        return carry

    def inverse_group(side):
        at = slice(128 * side, 128 * side + 128)

        def one(g, carry):
            v = inner(prod[g], slice(256 * side, 256 * side + 256))
            for i in range(0, GROUP, 2):
                pair = []
                for c in (i, i + 1):
                    re, im = v[64 * c : 64 * c + 64, :128], -v[64 * c : 64 * c + 64, 128:]
                    tr, ti = turn[0, :, at], turn[1, :, at]
                    pair.append(jnp.concatenate([re * tr + im * ti, im * tr - re * ti], axis=0))
                high = jnp.concatenate(pair, axis=1).astype(BF)
                y = jnp.dot(back[...], jnp.concatenate([high, high], axis=0), preferred_element_type=F32)
                out32[side, pl.ds(g * GROUP + i, 64, stride=16), :] = y[:, :128]
                out32[side, pl.ds(g * GROUP + i + 1, 64, stride=16), :] = y[:, 128:]
            return carry

        return one

    own_f.wait()
    from_owners(frecv, 1)
    widen(frecv[...])
    lax.fori_loop(0, 16 // GROUP, filter_group, 0)
    own_d.wait()
    pltpu.make_async_copy(drecv.at[pl.ds(0, 7)], drecv.at[pl.ds(0, 7)], all_recv.at[0]).wait()
    widen(drecv[...].reshape(64, 16, BLK))
    lax.fori_loop(0, 16 // GROUP, signal_group, 0)

    slot = mine * NZ + z
    own_c = []
    for side in range(2):
        lax.fori_loop(0, 16 // GROUP, inverse_group(side), 0)
        osend[side] = out32[side].reshape(64, 16, 128).astype(BF)

        own_c.append(
            to_owners(
                lambda yt, xt, zt, side=side: osend.at[side, zt * 8 + yt * NX + xt],
                crecv.at[side, slot],
                2 + side,
            )
        )

    own_q.wait()
    for copy in q_in:
        copy.wait_recv()
    for copy in own_o:
        copy.wait()

    far_h, near_h = (1 - yh) * 2, yh * 2
    p_in, y_copy = {}, {}
    for side in range(2):
        own_c[side].wait()
        from_owners(crecv.at[side], 2 + side)
        query = qrecv[:, :, 128 * side : 128 * side + 128].reshape(1024, 128).astype(F32)
        gated = (query * crecv[side].reshape(1024, 128).astype(F32)).T.astype(BF)

        def partial(h, half):
            return jnp.dot(gated, obuf[h, :, 512 * half : 512 * half + 512], preferred_element_type=F32)

        def swap(part, half, h):
            psend[side, part, half] = partial(h, half).astype(BF)
            p_in[side, part, half] = go.start(
                psend.at[side, part, half], precv.at[side, part, half], mate
            )

        swap(0, 0, far_h + 1 - core)
        total = partial(far_h + core, 0)
        swap(0, 1, far_h + 1 - core)
        for half in range(2):
            p_in[side, 0, half].wait_recv()
            ysend[side, half] = (total + precv[side, 0, half].astype(F32)).astype(BF)
            y_copy[side, half] = go.start(ysend.at[side, half], yrecv.at[side, half], across)
            if half == 0:
                total = partial(far_h + core, 1)
        for half in range(2):
            swap(1, half, near_h + 1 - core)
        for half in range(2):
            held[side, half] = partial(near_h + core, half)
    for side in range(2):
        for half in range(2):
            p_in[side, 1, half].wait_recv()
            y_copy[side, half].wait_recv()
            total = held[side, half] + precv[side, 1, half].astype(F32) + yrecv[side, half].astype(F32)
            out[pl.ds(128 * side, 128), pl.ds(512 * half, 512)] = total.astype(BF)

    go.wait_sends()
    pltpu.make_async_copy(drv.at[pl.ds(0, 7)], drv.at[pl.ds(0, 7)], all_send.at[0]).wait()
    pltpu.make_async_copy(frecv.at[pl.ds(0, 63)], frecv.at[pl.ds(0, 63)], all_send.at[1]).wait()
    for side in range(2):
        part = osend.at[side, pl.ds(0, 63)]
        pltpu.make_async_copy(part, part, all_send.at[2 + side]).wait()


def layer(act, w, taps, flt, w_out):
    any_space, vmem = pl.BlockSpec(memory_space=pl.ANY), pl.BlockSpec(memory_space=pltpu.VMEM)
    return pl.pallas_call(
        layer_kernel,
        out_shape=jax.ShapeDtypeStruct((BLK, 1024), BF),
        in_specs=[any_space] * 9,
        out_specs=vmem,
        scratch_shapes=[
            pltpu.VMEM((3, TAPS, 1024), F32),
            pltpu.VMEM((128, 128), BF),
            pltpu.VMEM((2, 64, BLK), F32),
            pltpu.VMEM((2 * BLK, 2 * BLK), BF),
            pltpu.VMEM((64, 256), BF),
            pltpu.VMEM((NY, NX, BLK, D), BF),
            pltpu.VMEM((NY, NX, NZ, DB, 3 * CG), BF),
            pltpu.VMEM((16, D), BF),
            pltpu.VMEM((16, 512), F32),
            pltpu.VMEM((16, 512), BF),
            pltpu.VMEM((NY, NX, 16, 512), BF),
            pltpu.VMEM((16, D), F32),
            pltpu.VMEM((8, 8, 3 * CG), F32),
            pltpu.VMEM((BLK + 8, 3 * CG), F32),
            pltpu.VMEM((1024, BLK), F32),
            pltpu.VMEM((8, NZ, 16, BLK), BF),
            pltpu.VMEM((64, 16, BLK), BF),
            pltpu.VMEM((NZ, 8, 16, BLK), BF),
            pltpu.VMEM((NZ, 8, 16, BLK), BF),
            pltpu.VMEM((8, CG, BLK), BF),
            pltpu.VMEM((8, CG, BLK), BF),
            pltpu.VMEM((2, 1024, 128), F32),
            pltpu.VMEM((2, 1024, 128), F32),
            pltpu.VMEM((16 // GROUP, 64 * GROUP, 2 * BLK), F32),
            pltpu.VMEM((16 // GROUP, 64 * GROUP, 2 * BLK), BF),
            pltpu.VMEM((2, 64, 16, 128), BF),
            pltpu.VMEM((2, 64, 16, 128), BF),
            pltpu.VMEM((4, 1024, 1024), BF),
            pltpu.VMEM((2, 2, 2, 128, 512), BF),
            pltpu.VMEM((2, 2, 2, 128, 512), BF),
            pltpu.VMEM((2, 2, 128, 512), BF),
            pltpu.VMEM((2, 2, 128, 512), BF),
            pltpu.VMEM((2, 2, 128, 512), F32),
            pltpu.SemaphoreType.DMA((16,)),
            pltpu.SemaphoreType.DMA((4,)),
            pltpu.SemaphoreType.DMA((4,)),
            pltpu.SemaphoreType.DMA((4,)),
            pltpu.SemaphoreType.DMA((N_COPIES,)),
            pltpu.SemaphoreType.DMA((N_COPIES,)),
        ],
        compiler_params=pltpu.CompilerParams(
            collective_id=0, has_side_effects=True, vmem_limit_bytes=58 * 1024 * 1024
        ),
        name="layer",
    )(act, w, taps, flt, w_out, *[jnp.asarray(table) for table in tables()])


def on_device(activations, w_in, short_taps, long_filter, w_out):
    return layer(activations, w_in, short_taps.transpose(0, 2, 1), long_filter, w_out)


def solution(mesh):
    return jax.shard_map(
        on_device,
        mesh=mesh,
        in_specs=(
            P("ctx", None),
            P(None, "ctx", "hid"),
            P(None, "hid", None),
            P("hid", "ctx"),
            P("hid", None),
        ),
        out_specs=P("ctx", "hid"),
        check_vma=False,
    )
```
